256 devices in a mesh: seq: 64 (over y, z_lo, x), chan: 4 (over z_hi, core).
Axes of the slice: x: 4, y: 4, z: 8 (z_hi: 2, z_lo: 4; z = z_hi * 4 + z_lo), core: 2. Of those that a mesh axis runs over, the one named last changes fastest.
Arguments:
- tokens: bfloat16 [131072, 1, 1536], P('seq', None, 'chan'), may hold values from -24 to 24
- norm_gain_seq: bfloat16 [1536], P('chan'), may hold values from 0.099609375 to 1.8984375
- seq_left: bfloat16 [512, 256, 256], P('seq'), may hold values from -0.375 to 0.375
- seq_right: bfloat16 [256, 512, 512], P('seq'), may hold values from -0.25 to 0.25
- norm_gain_mlp: bfloat16 [1536], P('chan'), may hold values from 0.099609375 to 1.8984375
- up_first: bfloat16 [2, 4, 384, 384], P(None, 'chan'), may hold values from -0.3125 to 0.3125
- up_second: bfloat16 [2, 4, 384, 1536], P(None, 'chan'), may hold values from -0.3125 to 0.3125
- down_first: bfloat16 [4, 1536, 384], P('chan'), may hold values from -0.15625 to 0.15625
- down_second: bfloat16 [4, 384, 384], P('chan'), may hold values from -0.3125 to 0.3125
Outputs:
- layer_out: bfloat16 [131072, 1, 1536], P('seq', None, 'chan')
The draws below stay inside these ranges and needn't reach their ends.
All inputs are finite; a program needn't handle non-finite values.
Results may differ from the reference program's by a relative error of at most 0.019.
Values may be sent and summed in bfloat16 or wider, within the bound.
A program may use at most 128 MiB of HBM per device.

```python
import math
import jax
import jax.numpy as jnp
from jax import lax

D = 1536
FF = 6144
BLOCKS = 4
OUTER = 512
INNER = 256
DOCS = 1
LENGTH = 131072


def draw_tokens(key, part):
    key = jax.random.fold_in(key, 11)
    key_base, key_cols, key_rows = jax.random.split(key, 3)
    shape = (LENGTH, DOCS, D)
    ramp = 3.0 ** (jnp.arange(D, dtype=jnp.float32) / D)
    col_scale = 0.3 * ramp * jnp.exp(jax.random.uniform(key_cols, (D,), jnp.float32, 0.0, math.log(3.3)))
    row_scale = jnp.exp(jax.random.uniform(key_rows, (LENGTH, DOCS, 1), jnp.float32, math.log(0.5), math.log(2.0)))
    base_values = jnp.clip(jax.random.normal(key_base, shape, jnp.float32), -4.0, 4.0)
    return (base_values * col_scale * row_scale).astype(jnp.bfloat16)


def block_scale(rng, extent, shards, low, top_value):
    level, own = 1.0, jax.random.fold_in(rng, 6)
    for position, blocks in shards:
        heights = jnp.exp(jax.random.uniform(jax.random.fold_in(own, position), (blocks,), jnp.float32, low / len(shards), top_value / len(shards)))
        level = level * jnp.repeat(heights, extent[position] // blocks).reshape([-1 if axis == position else 1 for axis in range(len(extent))])
    return level


def centred(stream_key, dims, scale, bound, cuts=(), held_as=jnp.bfloat16):
    result = scale * jax.random.normal(stream_key, dims, jnp.float32)
    if cuts:
        result = result * block_scale(stream_key, dims, cuts, -0.22, 0.18)
    return jnp.clip(result, -bound, bound).astype(held_as)


def setup_inputs(seed: int = 0) -> dict:
    seeds = jax.random.split(jax.random.key(seed), 10)
    return {
        "tokens": draw_tokens(jax.random.fold_in(seeds[9], 71), 0),
        "norm_gain_seq": jnp.clip(1.0 + 0.18 * jax.random.normal(seeds[1], (D,), jnp.float32), 0.099609375, 1.8984375).astype(jnp.bfloat16),
        "seq_left": centred(seeds[2], (OUTER, INNER, INNER), INNER ** -0.5, 0.375, ((0, 64),)),
        "seq_right": centred(seeds[3], (INNER, OUTER, OUTER), OUTER ** -0.5, 0.25, ((0, 64),)),
        "norm_gain_mlp": jnp.clip(1.0 + 0.18 * jax.random.normal(seeds[4], (D,), jnp.float32), 0.099609375, 1.8984375).astype(jnp.bfloat16),
        "up_first": centred(seeds[5], (2, BLOCKS, D // BLOCKS, D // BLOCKS), (D // BLOCKS) ** -0.5, 0.3125, ((1, 4),)),
        "up_second": centred(seeds[6], (2, BLOCKS, D // BLOCKS, FF // BLOCKS), (D // BLOCKS) ** -0.5, 0.3125, ((1, 4),)),
        "down_first": centred(seeds[7], (BLOCKS, FF // BLOCKS, D // BLOCKS), (FF // BLOCKS) ** -0.5, 0.15625, ((0, 4),)),
        "down_second": centred(seeds[8], (BLOCKS, D // BLOCKS, D // BLOCKS), (D // BLOCKS) ** -0.5, 0.3125, ((0, 4),)),
    }


def rms_scale(values, gain):
    mean_square = lax.optimization_barrier(jnp.mean(values * values, axis=-1, keepdims=True))
    return values * lax.rsqrt(mean_square + 1e-06) * gain.astype(jnp.float32)

def reference(tokens, norm_gain_seq, seq_left, seq_right, norm_gain_mlp, up_first, up_second, down_first, down_second):
    tokens_float = tokens.astype(jnp.float32)
    normed = rms_scale(tokens_float, norm_gain_seq).astype(jnp.bfloat16)
    total_width = DOCS * D
    flat_view = normed.reshape(OUTER, INNER, total_width)
    left_float = seq_left.astype(jnp.float32)
    right_float = seq_right.astype(jnp.float32)
    block_width = D // BLOCKS
    pieces = []
    for column_start in range(0, total_width, block_width):
        column_part = flat_view[:, :, column_start:column_start + block_width].astype(jnp.float32)
        first_section = jnp.einsum('aob,abc->aoc', left_float, column_part).astype(jnp.bfloat16)
        second_section = jnp.einsum('boa,abc->obc', right_float, first_section.astype(jnp.float32)).astype(jnp.bfloat16)
        pieces.append(second_section)
    seq_mixed = jnp.concatenate(pieces, axis=2).reshape(LENGTH, DOCS, D)
    stream = (tokens_float + seq_mixed.astype(jnp.float32) * normed.astype(jnp.float32)).astype(jnp.bfloat16)
    normed2 = rms_scale(stream.astype(jnp.float32), norm_gain_mlp).astype(jnp.bfloat16)
    total_rows = LENGTH * DOCS
    block_rows = math.gcd(total_rows, 4096)
    quarter = block_width // BLOCKS
    hidden_width = FF // BLOCKS
    up_one = up_first.astype(jnp.float32)
    up_two = up_second.astype(jnp.float32)
    down_one = down_first.astype(jnp.float32)
    down_two = down_second.astype(jnp.float32)

    def mlp_block(row_block):
        split_rows = row_block.reshape(block_rows, BLOCKS, block_width).astype(jnp.float32)
        projected = jnp.einsum('tij,gijk->gtik', split_rows, up_one).astype(jnp.bfloat16)
        projected = projected.reshape(2, block_rows, BLOCKS, BLOCKS, quarter).transpose(0, 1, 3, 2, 4)
        projected = projected.reshape(2, block_rows, BLOCKS, block_width)
        gate_up = jnp.einsum('gtpm,gpmn->gtpn', projected.astype(jnp.float32), up_two)
        hidden = (jax.nn.silu(gate_up[0]) * gate_up[1]).astype(jnp.bfloat16)
        down_rows = jnp.einsum('tpn,pnm->tpm', hidden.astype(jnp.float32), down_one).astype(jnp.bfloat16)
        down_rows = down_rows.reshape(block_rows, BLOCKS, BLOCKS, quarter).transpose(0, 2, 1, 3)
        down_rows = down_rows.reshape(block_rows, BLOCKS, block_width)
        block_out = jnp.einsum('trm,rmo->tro', down_rows.astype(jnp.float32), down_two)
        return block_out.reshape(block_rows, D)
    mlp_out = lax.map(mlp_block, normed2.reshape(total_rows // block_rows, block_rows, D))
    layer_out = stream.reshape(total_rows, D).astype(jnp.float32) + mlp_out.reshape(total_rows, D)
    return layer_out.astype(jnp.bfloat16).reshape(LENGTH, DOCS, D)
```

```python
import jax
import jax.numpy as jnp
from jax import lax
from jax.experimental import pallas as pl
from jax.experimental.pallas import tpu as pltpu
from jax.sharding import PartitionSpec as P

MESH = pl.DeviceIdType.MESH
BF16 = jnp.bfloat16
F32 = jnp.float32
W = 384
EPS = 1e-6


def dot(a, b):
    return jnp.dot(a, b, preferred_element_type=F32)


def remote(src, dst, send, recv, device):
    return pltpu.make_async_remote_copy(
        src_ref=src, dst_ref=dst, send_sem=send, recv_sem=recv, device_id=device, device_id_type=MESH
    )


def drain(ref, sem):
    pltpu.make_async_copy(ref, ref, sem).wait()


def layer_kernel(
    tok_in, gains_in, left_in, right_in, upf_in, ups_in, dnf_in, dns_in,
    out,
    X, GS, GM, SL, SR, SQ, RR, RC, FS, S1, R1, GB, S2, R2, ST, TS, OB, UF, US, DF, DS,
    ld, sq_sem, gm_sem, a1_sem, a2_sem, st_sem, out_send, out_recv, w1_send, w1_recv, wr_send, wr_recv, sib_send, sib_recv,
):
    s = lax.axis_index("seq")
    ch = lax.axis_index("chan")
    y, l, x = s // 16, (s // 4) % 4, s % 4
    sib = ch + 1 - 2 * (ch % 2)
    opp = (ch + 2) % 4

    def seq_of(yy, ll, xx):
        return yy * 16 + ll * 4 + xx

    mirror = (seq_of(y, 3 - l, x), opp)
    x_plus, x_minus = (seq_of(y, l, (x + 1) % 4), ch), (seq_of(y, l, (x + 3) % 4), ch)
    y_plus, y_minus = (seq_of((y + 1) % 4, l, x), ch), (seq_of((y + 3) % 4, l, x), ch)

    bar = pltpu.get_barrier_semaphore()

    @pl.loop(1, 64)
    def _(k):
        pl.semaphore_signal(bar, inc=1, device_id=((s + k) % 64, ch), device_id_type=MESH)

    @pl.loop(1, 4)
    def _(k):
        pl.semaphore_signal(bar, inc=1, device_id=(s, (ch + k) % 4), device_id_type=MESH)

    pl.semaphore_signal(bar, inc=1, device_id=mirror, device_id_type=MESH)

    loads = [
        pltpu.make_async_copy(tok_in, X, ld.at[0]),
        pltpu.make_async_copy(gains_in.at[0], GS, ld.at[1]),
        pltpu.make_async_copy(gains_in.at[1], GM.at[ch], ld.at[2]),
        pltpu.make_async_copy(left_in, SL, ld.at[3]),
        pltpu.make_async_copy(right_in, SR, ld.at[4]),
        pltpu.make_async_copy(ups_in, US.at[ch, :, pl.ds(0, 96)], ld.at[5]),
        pltpu.make_async_copy(upf_in, UF.at[ch], ld.at[6]),
        pltpu.make_async_copy(dnf_in, DF.at[ch], ld.at[7]),
        pltpu.make_async_copy(dns_in, DS.at[ch, :, pl.ds(0, 96)], ld.at[8]),
    ]
    for c in loads:
        c.start()

    eye = lax.broadcasted_iota(jnp.int32, (128, 128), 0) == lax.broadcasted_iota(jnp.int32, (128, 128), 1)
    loads[0].wait()

    @pl.loop(0, 16)
    def _(k):
        xb = X[pl.ds(pl.multiple_of(k * 128, 128), 128), :].astype(F32)
        col = jnp.sum(xb * xb, axis=1, keepdims=True)
        SQ[ch, pl.ds(k, 1), :] = jnp.sum(jnp.where(eye, col, 0.0), axis=0, keepdims=True)

    loads[2].wait()
    pl.semaphore_wait(bar, 67)

    @pl.loop(1, 4)
    def _(k):
        to = (s, (ch + k) % 4)
        remote(SQ.at[ch], SQ.at[ch], sq_sem.at[0], sq_sem.at[1], to).start()
        remote(GM.at[ch], GM.at[ch], gm_sem.at[0], gm_sem.at[1], to).start()

    ux = y * 4 + x
    uy = x * 4 + y

    def us_unit(blk, u, lanes=pl.ds(0, 1536)):
        return US.at[blk, u // 2, pl.ds(pl.multiple_of((u % 2) * 48, 16), 48), lanes]

    def us_row(blk, r, lanes=pl.ds(0, 1536)):
        return US.at[blk, pl.ds(r * 2, 2), pl.ds(0, 96), lanes]

    def uf_unit(blk, u, lanes=pl.ds(0, 512)):
        return UF.at[blk, pl.ds(pl.multiple_of(u * 48, 16), 48), lanes]

    def uf_row(blk, r, lanes=pl.ds(0, 512)):
        return UF.at[blk, pl.ds(pl.multiple_of(r * 192, 16), 192), lanes]

    def df_unit(blk, u, lanes=pl.ds(0, 512)):
        return DF.at[blk, pl.ds(pl.multiple_of(u * 96, 16), 96), lanes]

    def df_row(blk, r, lanes=pl.ds(0, 512)):
        return DF.at[blk, pl.ds(pl.multiple_of(r * 384, 16), 384), lanes]

    first_unit = [
        remote(ups_in.at[ux // 2, pl.ds(pl.multiple_of((ux % 2) * 48, 16), 48)], us_unit(ch, ux), w1_send.at[0], w1_recv.at[0], mirror),
        remote(upf_in.at[pl.ds(pl.multiple_of(uy * 48, 16), 48)], uf_unit(ch, uy), w1_send.at[1], w1_recv.at[1], mirror),
        remote(dnf_in.at[pl.ds(pl.multiple_of(uy * 96, 16), 96)], df_unit(ch, uy), w1_send.at[2], w1_recv.at[2], mirror),
        remote(dns_in, DS.at[ch, :, pl.ds(0, 96)], w1_send.at[3], w1_recv.at[3], mirror),
    ]
    for c in first_unit:
        c.start()

    to_sib = (s, sib)
    own_block = [
        remote(ups_in, US.at[ch, :, pl.ds(0, 96)], sib_send.at[0], sib_recv.at[0], to_sib),
        remote(upf_in, UF.at[ch], sib_send.at[1], sib_recv.at[1], to_sib),
        remote(dnf_in, DF.at[ch], sib_send.at[2], sib_recv.at[2], to_sib),
        remote(dns_in, DS.at[ch, :, pl.ds(0, 96)], sib_send.at[3], sib_recv.at[3], to_sib),
    ]
    other_block = [
        remote(US.at[opp, :, pl.ds(0, 96)], US.at[opp, :, pl.ds(0, 96)], sib_send.at[4], sib_recv.at[4], to_sib),
        remote(UF.at[opp], UF.at[opp], sib_send.at[5], sib_recv.at[5], to_sib),
        remote(DF.at[opp], DF.at[opp], sib_send.at[6], sib_recv.at[6], to_sib),
        remote(DS.at[opp, :, pl.ds(0, 96)], DS.at[opp, :, pl.ds(0, 96)], sib_send.at[7], sib_recv.at[7], to_sib),
    ]
    for c in own_block:
        c.start()

    xring, yring = (x, x_plus, x_minus), (y, y_plus, y_minus)
    ux_of = (lambda p: y * 4 + p, lambda p: p)
    uy_of = (lambda p: x * 4 + p, lambda p: p)
    tables = [
        (us_unit, us_row, 768, xring, yring, ux_of),
        (uf_unit, uf_row, 256, yring, xring, uy_of),
        (df_unit, df_row, 256, yring, xring, uy_of),
    ]

    def ring_copies(stage, step):
        copies = []
        for j, (unit, row, half, ring_a, ring_b, (first, second)) in enumerate(tables):
            pos, plus, minus = (ring_a, ring_b)[stage]
            part, index = ((unit, first), (row, second))[stage]
            sem = ((j * 2 + stage) * 2 + step) * 2
            if step == 0:
                mine = part(opp, index(pos))
                copies += [
                    remote(mine, mine, wr_send.at[sem], wr_recv.at[sem], plus),
                    remote(mine, mine, wr_send.at[sem + 1], wr_recv.at[sem + 1], minus),
                ]
            else:
                below = part(opp, index((pos + 3) % 4), pl.ds(0, half))
                above = part(opp, index((pos + 1) % 4), pl.ds(half, half))
                copies += [
                    remote(below, below, wr_send.at[sem], wr_recv.at[sem], plus),
                    remote(above, above, wr_send.at[sem + 1], wr_recv.at[sem + 1], minus),
                ]
        return copies

    rings = [ring_copies(0, 0), ring_copies(0, 1), ring_copies(1, 0), ring_copies(1, 1)]

    US[:, :, pl.ds(96, 32), :] = jnp.zeros((4, 8, 32, 1536), BF16)
    DS[:, :, pl.ds(96, 32), :] = jnp.zeros((4, 4, 32, W), BF16)

    drain(SQ.at[pl.ds(0, 3)], sq_sem.at[1])
    scale = lax.rsqrt((SQ[0] + SQ[1] + SQ[2] + SQ[3]) / 1536.0 + EPS)
    RR[...] = scale
    for c in (loads[1], loads[3]):
        c.wait()
    gain = GS[pl.ds(0, 1), :].astype(F32)

    @pl.loop(0, 8)
    def _(o):
        r = jnp.concatenate([RR[pl.ds(2 * o, 1), :], RR[pl.ds(2 * o + 1, 1), :]], axis=1)
        lw = (SL[o].astype(F32) * r).astype(BF16)
        rows = X[pl.ds(pl.multiple_of(o * 256, 256), 256), :]
        FS[o] = (dot(lw, rows) * gain).astype(BF16)

    out_row = lax.broadcasted_iota(jnp.int32, (256, 256), 0)
    in_row = lax.broadcasted_iota(jnp.int32, (256, 256), 1)
    perm = (in_row == (out_row & 7) * 32 + (out_row >> 5) * 4 + ((out_row >> 3) & 3)).astype(F32).astype(BF16)
    back = (out_row == (in_row & 7) * 32 + (in_row >> 5) * 4 + ((in_row >> 3) & 3)).astype(F32).astype(BF16)

    def a2a_send(src, dst, sems, d):
        @pl.when(d != s)
        def _():
            remote(src.at[d], dst.at[s], sems.at[0], sems.at[1], (d, ch)).start()

    @pl.loop(0, 8)
    def _(k):
        g = (k + s // 8) % 8
        block = FS[:, pl.ds(pl.multiple_of(g * 32, 32), 32), :].reshape(256, W)
        S1[pl.ds(g * 8, 8)] = dot(perm, block).astype(BF16).reshape(8, 32, W)

        @pl.loop(0, 8)
        def _(j):
            a2a_send(S1, R1, a1_sem, g * 8 + (j + s) % 8)

    R1[s] = S1[s]
    for c in first_unit:
        c.wait_recv()
    for c in rings[0]:
        c.start()

    @pl.loop(0, 16)
    def _(k):
        col = jnp.sum(jnp.where(eye, RR[pl.ds(k, 1), :], 0.0), axis=1, keepdims=True)
        RC[pl.ds(pl.multiple_of(k * 128, 128), 128), :] = jnp.broadcast_to(col, (128, 128))

    loads[4].wait()
    drain(R1.at[pl.ds(0, 63)], a1_sem.at[1])
    for c in rings[0]:
        c.wait_recv()
    for c in rings[1]:
        c.start()

    @pl.loop(0, 8)
    def _(g):
        part = R1[pl.ds(g * 8, 8)].astype(F32)
        for b in range(4):
            rows = part[:, 8 * b : 8 * b + 8, :].reshape(64, W)
            GB[b, pl.ds(pl.multiple_of(g * 64, 64), 64), :] = rows.astype(BF16)

    @pl.loop(0, 2)
    def _(k):
        m = (k + s // 32) % 2
        for pair in range(2):
            halves = [
                dot(SR[b, pl.ds(pl.multiple_of(m * 256, 256), 256), :], GB[b]).reshape(32, 8, W)
                for b in (2 * pair, 2 * pair + 1)
            ]
            S2[pl.ds(m * 32, 32), pl.ds(16 * pair, 16), :] = jnp.concatenate(halves, axis=1).astype(BF16)

        @pl.loop(0, 32)
        def _(j):
            a2a_send(S2, R2, a2_sem, m * 32 + (j + s) % 32)

    R2[s] = S2[s]
    for c in rings[1]:
        c.wait_recv()
    for c in rings[2]:
        c.start()
    drain(R2.at[pl.ds(0, 63)], a2_sem.at[1])

    @pl.loop(0, 8)
    def _(g):
        mixed = dot(back, R2[pl.ds(g * 8, 8)].reshape(256, W)).reshape(8, 32, W)
        for o in range(8):
            at = pl.ds(pl.multiple_of(o * 256 + g * 32, 32), 32)
            rc = RC[at, :]
            xs = X[at, :].astype(F32)
            normed = (xs * jnp.concatenate([rc, rc, rc], axis=1) * gain).astype(BF16).astype(F32)
            ST[at, :] = (xs + mixed[o] * normed).astype(BF16)

    @pl.loop(1, 4)
    def _(k):
        q = (ch + k) % 4
        remote(ST.at[pl.ds(pl.multiple_of(q * 512, 512), 512)], TS.at[ch], st_sem.at[0], st_sem.at[1], (s, q)).start()

    TS[ch] = ST[pl.ds(pl.multiple_of(ch * 512, 512), 512), :]
    for c in rings[2]:
        c.wait_recv()
    for c in rings[3]:
        c.start()
    for c in rings[3]:
        c.wait_recv()
    for c in other_block:
        c.start()
    for c in loads[5:]:
        c.wait()
    drain(GM.at[pl.ds(0, 3)], gm_sem.at[1])
    for c in own_block:
        c.wait_recv()
    drain(TS.at[pl.ds(0, 3)], st_sem.at[1])
    for c in other_block:
        c.wait_recv()

    @pl.loop(0, 2)
    def _(t):
        at = pl.ds(pl.multiple_of(t * 256, 256), 256)
        squares = jnp.zeros((256, 1), F32)
        for i in range(4):
            v = TS[i, at, :].astype(F32)
            squares += jnp.sum(v * v, axis=1, keepdims=True)
        r2 = lax.rsqrt(squares / 1536.0 + EPS)
        projected = []
        for i in range(4):
            n = (TS[i, at, :].astype(F32) * r2 * GM[i, pl.ds(0, 1), :].astype(F32)).astype(BF16)
            projected.append([dot(n, UF[i, pl.ds(g * W, W), :]).astype(BF16) for g in range(2)])
        down = []
        for p in range(4):
            merged = [
                jnp.concatenate([projected[i][g][:, p * 128 : p * 128 + 128] for i in range(4)], axis=1) for g in range(2)
            ]
            acc = jnp.zeros((256, 512), F32)
            for n in range(3):
                lanes = pl.ds(n * 512, 512)
                gate, up = (dot(merged[g], US[p, pl.ds(g * 4, 4), :, lanes].reshape(512, 512)) for g in range(2))
                hidden = (gate / (1.0 + jnp.exp(-gate)) * up).astype(BF16)
                acc += dot(hidden, DF[p, pl.ds(n * 512, 512), :])
            down.append(acc.astype(BF16))
        for r in range(4):
            merged = jnp.concatenate([down[p][:, r * 128 : r * 128 + 128] for p in range(4)], axis=1)
            mlp = dot(merged, DS[r].reshape(512, W))
            OB[r, at, :] = (TS[r, at, :].astype(F32) + mlp).astype(BF16)
        home = pl.ds(pl.multiple_of(ch * 512 + t * 256, 256), 256)
        out[home, :] = OB[ch, at, :]

        @pl.loop(1, 4)
        def _(k):
            r = (ch + k) % 4
            remote(OB.at[r, at], out.at[home], out_send.at[t], out_recv.at[t], (s, r)).start()

    drain(SQ.at[pl.ds(0, 3)], sq_sem.at[0])
    drain(GM.at[pl.ds(0, 3)], gm_sem.at[0])
    drain(S1.at[pl.ds(0, 63)], a1_sem.at[0])
    drain(S2.at[pl.ds(0, 63)], a2_sem.at[0])
    drain(TS.at[pl.ds(0, 3)], st_sem.at[0])
    for c in first_unit + own_block + other_block + rings[0] + rings[1] + rings[2] + rings[3]:
        c.wait_send()
    for t in range(2):
        drain(out.at[pl.ds(0, 768)], out_send.at[t])
        drain(out.at[pl.ds(0, 768)], out_recv.at[t])


def on_device(
    tokens, norm_gain_seq, seq_left, seq_right, norm_gain_mlp, up_first, up_second, down_first, down_second
):
    rows = tokens.shape[0]
    gains = jnp.broadcast_to(jnp.stack([norm_gain_seq, norm_gain_mlp])[:, None, :], (2, 16, W))
    upf = jnp.pad(up_first.reshape(768, 4, 96), ((0, 0), (0, 0), (0, 32))).reshape(768, 512)
    dnf = jnp.pad(down_first.reshape(1536, 4, 96), ((0, 0), (0, 0), (0, 32))).reshape(1536, 512)
    hbm = pl.BlockSpec(memory_space=pl.ANY)
    dma = pltpu.SemaphoreType.DMA
    out = pl.pallas_call(
        layer_kernel,
        out_shape=jax.ShapeDtypeStruct((rows, W), BF16),
        in_specs=[hbm] * 8,
        out_specs=pl.BlockSpec(memory_space=pltpu.VMEM),
        scratch_shapes=[
            pltpu.VMEM((2048, W), BF16),
            pltpu.VMEM((16, W), BF16),
            pltpu.VMEM((4, 16, W), BF16),
            pltpu.VMEM((8, 256, 256), BF16),
            pltpu.VMEM((4, 512, 512), BF16),
            pltpu.VMEM((4, 16, 128), F32),
            pltpu.VMEM((16, 128), F32),
            pltpu.VMEM((2048, 128), F32),
            pltpu.VMEM((8, 256, W), BF16),
            pltpu.VMEM((64, 32, W), BF16),
            pltpu.VMEM((64, 32, W), BF16),
            pltpu.VMEM((4, 512, W), BF16),
            pltpu.VMEM((64, 32, W), BF16),
            pltpu.VMEM((64, 32, W), BF16),
            pltpu.VMEM((2048, W), BF16),
            pltpu.VMEM((4, 512, W), BF16),
            pltpu.VMEM((4, 512, W), BF16),
            pltpu.VMEM((4, 768, 512), BF16),
            pltpu.VMEM((4, 8, 128, 1536), BF16),
            pltpu.VMEM((4, 1536, 512), BF16),
            pltpu.VMEM((4, 4, 128, W), BF16),
            dma((9,)), dma((2,)), dma((2,)), dma((2,)), dma((2,)), dma((2,)), dma((2,)), dma((2,)),
            dma((4,)), dma((4,)), dma((24,)), dma((24,)), dma((8,)), dma((8,)),
        ],
        compiler_params=pltpu.CompilerParams(
            collective_id=0, has_side_effects=True, vmem_limit_bytes=60 * 2**20
        ),
        name="layer",
    )(
        tokens.reshape(rows, W), gains, seq_left, seq_right, upf,
        up_second.reshape(8, 96, 1536), dnf, down_second.reshape(4, 96, W),
    )
    return out.reshape(rows, 1, W)


def solution(mesh):
    return jax.shard_map(
        on_device,
        mesh=mesh,
        in_specs=(
            P("seq", None, "chan"),
            P("chan"),
            P("seq", None, None),
            P("seq", None, None),
            P("chan"),
            P(None, "chan", None, None),
            P(None, "chan", None, None),
            P("chan", None, None),
            P("chan", None, None),
        ),
        out_specs=P("seq", None, "chan"),
        check_vma=False,
    )
```

```python
import jax
import jax.numpy as jnp
from jax import lax
from jax.experimental import pallas as pl
from jax.experimental.pallas import tpu as pltpu
from jax.sharding import PartitionSpec as P

MESH = pl.DeviceIdType.MESH
BF16 = jnp.bfloat16
F32 = jnp.float32
W = 384
EPS = 1e-6


def dot(a, b):
    return jnp.dot(a, b, preferred_element_type=F32)


def remote(src, dst, send, recv, device):
    return pltpu.make_async_remote_copy(
        src_ref=src, dst_ref=dst, send_sem=send, recv_sem=recv, device_id=device, device_id_type=MESH
    )


def drain(ref, sem):
    pltpu.make_async_copy(ref, ref, sem).wait()


def layer_kernel(
    tok_in, gseq_in, gmlp_in, left_in, right_in, upf_in, ups_in, dnf_in, dns_in,
    out,
    X, G, SL, SR, SQ, RR, RC, FS, S1, R1, GB, S2, R2, MB, XB, ST, TS, OB, UF, US, DF, DS, UR, DR,
    ld, sq_sem, gm_sem, xb_sem, a1_sem, a2_sem, mb_sem, st_sem, out_send, out_recv, w1_send, w1_recv, wr_send, wr_recv, sib_send, sib_recv,
):
    s = lax.axis_index("seq")
    ch = lax.axis_index("chan")
    y, l, x = s // 16, (s // 4) % 4, s % 4
    sib = ch + 1 - 2 * (ch % 2)
    opp = (ch + 2) % 4
    h, c = ch // 2, ch % 2
    side = l // 2
    far = 2 * (1 - h)

    def seq_of(yy, ll, xx):
        return yy * 16 + ll * 4 + xx

    mirror = (seq_of(y, 3 - l, x), opp)
    x_plus, x_minus = (seq_of(y, l, (x + 1) % 4), ch), (seq_of(y, l, (x + 3) % 4), ch)
    y_plus, y_minus = (seq_of((y + 1) % 4, l, x), ch), (seq_of((y + 3) % 4, l, x), ch)

    bar = pltpu.get_barrier_semaphore()

    @pl.loop(1, 64)
    def _(k):
        pl.semaphore_signal(bar, inc=1, device_id=((s + k) % 64, ch), device_id_type=MESH)

    @pl.loop(1, 4)
    def _(k):
        pl.semaphore_signal(bar, inc=1, device_id=(s, (ch + k) % 4), device_id_type=MESH)

    pl.semaphore_signal(bar, inc=1, device_id=mirror, device_id_type=MESH)

    @pl.loop(0, 32)
    def _(k):
        sender = seq_of(2 * c + k // 16, 2 * (1 - side) + (k // 8) % 2, (k // 2) % 4)
        pl.semaphore_signal(bar, inc=1, device_id=(sender, far + k % 2), device_id_type=MESH)

    loads = [
        pltpu.make_async_copy(tok_in, X, ld.at[0]),
        pltpu.make_async_copy(upf_in, UR, ld.at[1]),
        pltpu.make_async_copy(dnf_in, DR, ld.at[2]),
        pltpu.make_async_copy(left_in, SL, ld.at[3]),
        pltpu.make_async_copy(right_in, SR, ld.at[4]),
        pltpu.make_async_copy(ups_in, US.at[ch, :, pl.ds(0, 96)], ld.at[5]),
        pltpu.make_async_copy(dns_in, DS.at[ch, :, pl.ds(0, 96)], ld.at[6]),
    ]
    for cp in loads:
        cp.start()

    eye = lax.broadcasted_iota(jnp.int32, (128, 128), 0) == lax.broadcasted_iota(jnp.int32, (128, 128), 1)
    loads[0].wait()

    @pl.loop(0, 16)
    def _(k):
        xb = X[k // 2, pl.ds(2 * (k % 2), 2)].reshape(128, W).astype(F32)
        col = jnp.sum(xb * xb, axis=1, keepdims=True)
        SQ[ch, pl.ds(k, 1), :] = jnp.sum(jnp.where(eye, col, 0.0), axis=0, keepdims=True)

    G[ch, 0] = jnp.broadcast_to(gseq_in[...].reshape(1, W), (16, W))
    G[ch, 1] = jnp.broadcast_to(gmlp_in[...].reshape(1, W), (16, W))
    pl.semaphore_wait(bar, 99)

    @pl.loop(1, 4)
    def _(k):
        to = (s, (ch + k) % 4)
        remote(SQ.at[ch], SQ.at[ch], sq_sem.at[0], sq_sem.at[1], to).start()
        remote(G.at[ch], G.at[ch], gm_sem.at[0], gm_sem.at[1], to).start()

    from_lane = lax.broadcasted_iota(jnp.int32, (W, 512), 0)
    to_lane = lax.broadcasted_iota(jnp.int32, (W, 512), 1)
    kept = ((to_lane & 127) < 96) & (from_lane == (to_lane >> 7) * 96 + (to_lane & 127))
    spread = kept.astype(F32).astype(BF16)
    loads[1].wait()
    loads[2].wait()

    @pl.loop(0, 3)
    def _(k):
        at = pl.ds(pl.multiple_of(k * 256, 256), 256)
        UF[ch, at, :] = dot(UR[at, :], spread).astype(BF16)

    @pl.loop(0, 6)
    def _(k):
        at = pl.ds(pl.multiple_of(k * 256, 256), 256)
        DF[ch, at, :] = dot(DR[at, :], spread).astype(BF16)

    ux = y * 4 + x
    uy = x * 4 + y

    def us_unit(blk, u, lanes=pl.ds(0, 1536)):
        return US.at[blk, u // 2, pl.ds(pl.multiple_of((u % 2) * 48, 16), 48), lanes]

    def us_row(blk, r, lanes=pl.ds(0, 1536)):
        return US.at[blk, pl.ds(r * 2, 2), pl.ds(0, 96), lanes]

    def uf_unit(blk, u, lanes=pl.ds(0, 512)):
        return UF.at[blk, pl.ds(pl.multiple_of(u * 48, 16), 48), lanes]

    def uf_row(blk, r, lanes=pl.ds(0, 512)):
        return UF.at[blk, pl.ds(pl.multiple_of(r * 192, 16), 192), lanes]

    def df_unit(blk, u, lanes=pl.ds(0, 512)):
        return DF.at[blk, pl.ds(pl.multiple_of(u * 96, 16), 96), lanes]

    def df_row(blk, r, lanes=pl.ds(0, 512)):
        return DF.at[blk, pl.ds(pl.multiple_of(r * 384, 16), 384), lanes]

    def ds_unit(blk, u, lanes=pl.ds(0, W)):
        return DS.at[blk, u, pl.ds(0, 96), lanes]

    first_unit = [
        remote(ups_in.at[ux // 2, pl.ds(pl.multiple_of((ux % 2) * 48, 16), 48)], us_unit(ch, ux), w1_send.at[0], w1_recv.at[0], mirror),
        remote(uf_unit(ch, uy), uf_unit(ch, uy), w1_send.at[1], w1_recv.at[1], mirror),
        remote(df_unit(ch, uy), df_unit(ch, uy), w1_send.at[2], w1_recv.at[2], mirror),
        remote(dns_in.at[x], ds_unit(ch, x), w1_send.at[3], w1_recv.at[3], mirror),
    ]
    for cp in first_unit:
        cp.start()

    tokens_across = [
        remote(X.at[pl.ds(2 * far, 4), pl.ds(2 * k, 2), 1 - side], XB.at[c], xb_sem.at[0], xb_sem.at[1], (s, far + k))
        for k in range(2)
    ]

    to_sib = (s, sib)
    own_block = [
        remote(ups_in, US.at[ch, :, pl.ds(0, 96)], sib_send.at[0], sib_recv.at[0], to_sib),
        remote(UF.at[ch], UF.at[ch], sib_send.at[1], sib_recv.at[1], to_sib),
        remote(DF.at[ch], DF.at[ch], sib_send.at[2], sib_recv.at[2], to_sib),
        remote(dns_in, DS.at[ch, :, pl.ds(0, 96)], sib_send.at[3], sib_recv.at[3], to_sib),
    ]
    other_block = [
        remote(US.at[opp, :, pl.ds(0, 96)], US.at[opp, :, pl.ds(0, 96)], sib_send.at[4], sib_recv.at[4], to_sib),
        remote(UF.at[opp], UF.at[opp], sib_send.at[5], sib_recv.at[5], to_sib),
        remote(DF.at[opp], DF.at[opp], sib_send.at[6], sib_recv.at[6], to_sib),
        remote(DS.at[opp, :, pl.ds(0, 96)], DS.at[opp, :, pl.ds(0, 96)], sib_send.at[7], sib_recv.at[7], to_sib),
    ]
    for cp in own_block:
        cp.start()

    xring, yring = (x, x_plus, x_minus), (y, y_plus, y_minus)
    ux_of = (lambda p: y * 4 + p, lambda p: p)
    uy_of = (lambda p: x * 4 + p, lambda p: p)
    tables = [
        (us_unit, us_row, 1536, xring, yring, ux_of),
        (uf_unit, uf_row, 512, yring, xring, uy_of),
        (df_unit, df_row, 512, yring, xring, uy_of),
        (ds_unit, None, 384, xring, None, (lambda p: p, None)),
    ]

    def ring_copies(stage, step):
        copies = []
        for j, (unit, row, width, ring_a, ring_b, (first, second)) in enumerate(tables):
            if stage and row is None:
                continue
            pos, plus, minus = (ring_a, ring_b)[stage]
            part, index = ((unit, first), (row, second))[stage]
            sem = ((j * 2 + stage) * 2 + step) * 2
            if step == 0:
                mine = part(opp, index(pos))
                copies += [
                    remote(mine, mine, wr_send.at[sem], wr_recv.at[sem], plus),
                    remote(mine, mine, wr_send.at[sem + 1], wr_recv.at[sem + 1], minus),
                ]
            else:
                half = width // 256 * 128
                below = part(opp, index((pos + 3) % 4), pl.ds(0, half))
                above = part(opp, index((pos + 1) % 4), pl.ds(half, width - half))
                copies += [
                    remote(below, below, wr_send.at[sem], wr_recv.at[sem], plus),
                    remote(above, above, wr_send.at[sem + 1], wr_recv.at[sem + 1], minus),
                ]
        return copies

    rings = [ring_copies(0, 0), ring_copies(0, 1), ring_copies(1, 0), ring_copies(1, 1)]

    US[:, :, pl.ds(96, 32), :] = jnp.zeros((4, 8, 32, 1536), BF16)
    DS[:, :, pl.ds(96, 32), :] = jnp.zeros((4, 4, 32, W), BF16)

    drain(SQ.at[pl.ds(0, 3)], sq_sem.at[1])
    scale = lax.rsqrt((SQ[0] + SQ[1] + SQ[2] + SQ[3]) / 1536.0 + EPS)
    RR[...] = scale
    loads[3].wait()
    gain = gseq_in[...].reshape(1, W).astype(F32)

    @pl.loop(0, 8, unroll=4)
    def _(o):
        r = jnp.concatenate([RR[pl.ds(2 * o, 1), :], RR[pl.ds(2 * o + 1, 1), :]], axis=1)
        lw = (SL[o].astype(F32) * r).astype(BF16)
        FS[o] = (dot(lw, X[o].reshape(256, W)) * gain).astype(BF16)

    out_row = lax.broadcasted_iota(jnp.int32, (256, 256), 0)
    in_row = lax.broadcasted_iota(jnp.int32, (256, 256), 1)
    perm = (in_row == (out_row & 7) * 32 + (out_row >> 5) * 4 + ((out_row >> 3) & 3)).astype(F32).astype(BF16)

    @pl.loop(0, 8)
    def _(k):
        g = (k + s // 8) % 8
        block = FS[:, pl.ds(pl.multiple_of(g * 32, 32), 32), :].reshape(256, W)
        S1[pl.ds(g * 8, 8)] = dot(perm, block).astype(BF16).reshape(8, 32, W)

        @pl.loop(0, 8)
        def _(j):
            d = g * 8 + (j + s) % 8

            @pl.when(d != s)
            def _():
                remote(S1.at[d], R1.at[s], a1_sem.at[0], a1_sem.at[1], (d, ch)).start()

    tokens_across[0].start()
    tokens_across[1].start()
    R1[s] = S1[s]

    @pl.loop(0, 16)
    def _(k):
        col = jnp.sum(jnp.where(eye, RR[pl.ds(k, 1), :], 0.0), axis=1, keepdims=True)
        RC[k // 2, pl.ds(2 * (k % 2), 2)] = jnp.broadcast_to(col, (128, 128)).reshape(2, 2, 32, 128)

    for cp in first_unit:
        cp.wait_recv()
    for cp in rings[0]:
        cp.start()
    for k in range(3):
        for cp in rings[k]:
            cp.wait_recv()
        for cp in rings[k + 1]:
            cp.start()
    loads[4].wait()
    drain(R1.at[pl.ds(0, 63)], a1_sem.at[1])

    @pl.loop(0, 8, unroll=2)
    def _(g):
        part = R1[pl.ds(g * 8, 8)].astype(F32)
        for b in range(4):
            rows = part[:, 8 * b : 8 * b + 8, :].reshape(64, W)
            GB[b, pl.ds(pl.multiple_of(g * 64, 64), 64), :] = rows.astype(BF16)

    low = lax.broadcasted_iota(jnp.int32, (32, 8, W), 1) < 4

    @pl.loop(0, 2)
    def _(k):
        m = (k + y // 2) % 2
        halves = ([], [])
        for pair in range(2):
            even, odd = (
                dot(SR[b, pl.ds(pl.multiple_of(m * 256, 256), 256), :], GB[b]).reshape(32, 8, W)
                for b in (2 * pair, 2 * pair + 1)
            )
            halves[0].append(jnp.where(low, even, pltpu.roll(odd, 4, 1)))
            halves[1].append(jnp.where(low, pltpu.roll(even, 4, 1), odd))
        for half in range(2):
            S2[pl.ds(m * 32, 32), half] = jnp.concatenate(halves[half], axis=1).astype(BF16)

        @pl.loop(0, 32)
        def _(j):
            d = m * 32 + (j + s) % 32
            same = (d // 8) % 2 == side

            @pl.when(same & (d != s))
            def _():
                remote(S2.at[d], R2.at[s], a2_sem.at[0], a2_sem.at[1], (d, ch)).start()

            @pl.when(jnp.logical_not(same))
            def _():
                remote(S2.at[d, h], R2.at[s, h], a2_sem.at[0], a2_sem.at[1], (d, ch)).start()
                remote(
                    S2.at[d, 1 - h], MB.at[c, y % 2, (l % 2) * 4 + x], mb_sem.at[0], mb_sem.at[1], (d, far + y // 2)
                ).start()

    R2[s] = S2[s]
    for cp in rings[3]:
        cp.wait_recv()
    for cp in other_block:
        cp.start()

    out_row = lax.broadcasted_iota(jnp.int32, (128, 128), 0)
    in_row = lax.broadcasted_iota(jnp.int32, (128, 128), 1)
    back = (in_row == ((out_row >> 2) & 7) * 16 + (out_row & 3) * 4 + (out_row >> 5)).astype(F32).astype(BF16)

    def streamed(xs, mixed, rc, gains):
        xs = xs.reshape(128, W).astype(F32)
        rc = rc.reshape(128, 128)
        normed = (xs * jnp.concatenate([rc, rc, rc], axis=1) * gains).astype(BF16).astype(F32)
        return (xs + dot(back, mixed.reshape(128, W)) * normed).astype(BF16).reshape(4, 32, W)

    def at_home(hh, yy, half):
        o4 = pl.ds(4 * hh, 4)
        mixed = R2[pl.ds(yy * 16 + half * 8, 8), hh]
        ST[o4, yy, half] = streamed(X[o4, yy, half], mixed, RC[o4, yy, half], gain)

    drain(R2.at[pl.ds(0, 47)], a2_sem.at[1])

    @pl.loop(0, 4, unroll=2)
    def _(yy):
        at_home(1 - h, yy, side)

    for t in range(2):
        for k in range(2):
            remote(
                ST.at[pl.ds(2 * far + 2 * t, 2), pl.ds(2 * k, 2), side],
                TS.at[ch, pl.ds(2 * t, 2), :, side],
                st_sem.at[0, t], st_sem.at[1, t], (s, far + k),
            ).start()

    @pl.loop(0, 8, unroll=2)
    def _(g):
        at_home(h, g // 2, g % 2)

    for t in range(2):
        remote(
            ST.at[pl.ds(4 * h + 2 * t, 2), pl.ds(2 * (1 - c), 2)], TS.at[ch, pl.ds(2 * t, 2)],
            st_sem.at[0, t], st_sem.at[1, t], to_sib,
        ).start()
    TS[ch] = ST[pl.ds(4 * h, 4), pl.ds(2 * c, 2)]

    drain(G.at[pl.ds(0, 3)], gm_sem.at[1])
    drain(XB, xb_sem.at[1])
    drain(MB, mb_sem.at[1])
    for k in range(2):
        gains = G[far + k, 0, pl.ds(0, 1), :].astype(F32)
        for yy in range(2):
            rc = RC[pl.ds(4 * h, 4), 2 * c + yy, 1 - side]
            TS[far + k, :, yy, 1 - side] = streamed(XB[k, :, yy], MB[k, yy], rc, gains)

    for cp in loads[5:]:
        cp.wait()
    for cp in own_block:
        cp.wait_recv()
    for cp in other_block:
        cp.wait_recv()

    def stream_of(i, at):
        return TS[i, at].reshape(256, W).astype(F32)

    @pl.loop(0, 2)
    def _(t):
        at = pl.ds(2 * t, 2)
        drain(TS.at[0], st_sem.at[1, t])
        squares = jnp.zeros((256, 1), F32)
        for i in range(4):
            v = stream_of(i, at)
            squares += jnp.sum(v * v, axis=1, keepdims=True)
        r2 = lax.rsqrt(squares / 1536.0 + EPS)
        projected = []
        for i in range(4):
            n = (stream_of(i, at) * r2 * G[i, 1, pl.ds(0, 1), :].astype(F32)).astype(BF16)
            projected.append([dot(n, UF[i, pl.ds(g * W, W), :]).astype(BF16) for g in range(2)])
        down = []
        for p in range(4):
            merged = [
                jnp.concatenate([projected[i][g][:, p * 128 : p * 128 + 128] for i in range(4)], axis=1) for g in range(2)
            ]
            acc = jnp.zeros((256, 512), F32)
            for n in range(3):
                lanes = pl.ds(n * 512, 512)
                gate, up = (dot(merged[g], US[p, pl.ds(g * 4, 4), :, lanes].reshape(512, 512)) for g in range(2))
                hidden = (gate / (1.0 + jnp.exp(-gate)) * up).astype(BF16)
                acc += dot(hidden, DF[p, pl.ds(n * 512, 512), :])
            down.append(acc.astype(BF16))
        for r in range(4):
            merged = jnp.concatenate([down[p][:, r * 128 : r * 128 + 128] for p in range(4)], axis=1)
            mlp = dot(merged, DS[r].reshape(512, W))
            OB[r, at] = (stream_of(r, at) + mlp).astype(BF16).reshape(2, 2, 2, 32, W)
        home = (pl.ds(4 * h + 2 * t, 2), pl.ds(2 * c, 2))
        for r in (far, far + 1, sib):
            remote(OB.at[r, at], out.at[home], out_send.at[t], out_recv.at[t], (s, r)).start()
        out[home] = OB[ch, at]

    drain(SQ.at[pl.ds(0, 3)], sq_sem.at[0])
    drain(G.at[pl.ds(0, 3)], gm_sem.at[0])
    drain(XB, xb_sem.at[0])
    drain(S1.at[pl.ds(0, 63)], a1_sem.at[0])
    drain(S2.at[pl.ds(0, 47)], a2_sem.at[0])
    drain(MB, mb_sem.at[0])
    for cp in first_unit + own_block + other_block + rings[0] + rings[1] + rings[2] + rings[3]:
        cp.wait_send()
    for t in range(2):
        drain(TS.at[0], st_sem.at[0, t])
        drain(out.at[pl.ds(0, 3)], out_send.at[t])
        drain(out.at[pl.ds(0, 3)], out_recv.at[t])


def on_device(
    tokens, norm_gain_seq, seq_left, seq_right, norm_gain_mlp, up_first, up_second, down_first, down_second
):
    rows = tokens.shape[0]
    hbm = pl.BlockSpec(memory_space=pl.ANY)
    vmem = pl.BlockSpec(memory_space=pltpu.VMEM)
    dma = pltpu.SemaphoreType.DMA
    out = pl.pallas_call(
        layer_kernel,
        out_shape=jax.ShapeDtypeStruct((8, 4, 2, 32, W), BF16),
        in_specs=[hbm, vmem, vmem] + [hbm] * 6,
        out_specs=pl.BlockSpec(memory_space=pltpu.VMEM),
        scratch_shapes=[
            pltpu.VMEM((8, 4, 2, 32, W), BF16),
            pltpu.VMEM((4, 2, 16, W), BF16),
            pltpu.VMEM((8, 256, 256), BF16),
            pltpu.VMEM((4, 512, 512), BF16),
            pltpu.VMEM((4, 16, 128), F32),
            pltpu.VMEM((16, 128), F32),
            pltpu.VMEM((8, 4, 2, 32, 128), F32),
            pltpu.VMEM((8, 256, W), BF16),
            pltpu.VMEM((64, 32, W), BF16),
            pltpu.VMEM((64, 32, W), BF16),
            pltpu.VMEM((4, 512, W), BF16),
            pltpu.VMEM((64, 2, 16, W), BF16),
            pltpu.VMEM((64, 2, 16, W), BF16),
            pltpu.VMEM((2, 2, 8, 16, W), BF16),
            pltpu.VMEM((2, 4, 2, 32, W), BF16),
            pltpu.VMEM((8, 4, 2, 32, W), BF16),
            pltpu.VMEM((4, 4, 2, 2, 32, W), BF16),
            pltpu.VMEM((4, 4, 2, 2, 32, W), BF16),
            pltpu.VMEM((4, 768, 512), BF16),
            pltpu.VMEM((4, 8, 128, 1536), BF16),
            pltpu.VMEM((4, 1536, 512), BF16),
            pltpu.VMEM((4, 4, 128, W), BF16),
            pltpu.VMEM((768, W), BF16),
            pltpu.VMEM((1536, W), BF16),
            dma((7,)), dma((2,)), dma((2,)), dma((2,)), dma((2,)), dma((2,)), dma((2,)), dma((2, 2)), dma((2,)), dma((2,)),
            dma((4,)), dma((4,)), dma((32,)), dma((32,)), dma((8,)), dma((8,)),
        ],
        compiler_params=pltpu.CompilerParams(
            collective_id=0, has_side_effects=True, vmem_limit_bytes=60 * 2**20
        ),
        name="layer",
    )(
        tokens.reshape(8, 4, 2, 32, W), norm_gain_seq, norm_gain_mlp, seq_left, seq_right, up_first.reshape(768, W),
        up_second.reshape(8, 96, 1536), down_first.reshape(1536, W), down_second.reshape(4, 96, W),
    )
    return out.reshape(rows, 1, W)


def solution(mesh):
    return jax.shard_map(
        on_device,
        mesh=mesh,
        in_specs=(
            P("seq", None, "chan"),
            P("chan"),
            P("seq", None, None),
            P("seq", None, None),
            P("chan"),
            P(None, "chan", None, None),
            P(None, "chan", None, None),
            P("chan", None, None),
            P("chan", None, None),
        ),
        out_specs=P("seq", None, "chan"),
        check_vma=False,
    )
```

```python
import jax
import jax.numpy as jnp
from jax import lax
from jax.experimental import pallas as pl
from jax.experimental.pallas import tpu as pltpu
from jax.sharding import PartitionSpec as P

MESH = pl.DeviceIdType.MESH
BF16 = jnp.bfloat16
F32 = jnp.float32
W = 384
EPS = 1e-6
PARTS = ((0, 256), (256, 128))


def dot(a, b):
    return jnp.dot(a, b, preferred_element_type=F32)


def remote(src, dst, send, recv, device):
    return pltpu.make_async_remote_copy(
        src_ref=src, dst_ref=dst, send_sem=send, recv_sem=recv, device_id=device, device_id_type=MESH
    )


def drain(ref, sem):
    pltpu.make_async_copy(ref, ref, sem).wait()


def layer_kernel(
    tok_in, gseq_in, gmlp_in, left_in, right_in, upf_in, ups_in, dnf_in, dns_in,
    out,
    X, G, SL, SR, SQ, RR, RC, FS0, FS1, S10, S11, R10, R11, GB0, GB1, S20, S21, R20, R21, MB0, MB1, XB, ST, TS, OB, UF, US, DF, DS, UR, DR,
    ld, sq_sem, gm_sem, xb_sem, a1_sem, a2_sem, mb_sem, st_sem, own_sem, out_send, out_recv, w1_send, w1_recv, wr_send, wr_recv, sib_send, sib_recv,
):
    FS, S1, R1, GB = (FS0, FS1), (S10, S11), (R10, R11), (GB0, GB1)
    S2, R2, MB = (S20, S21), (R20, R21), (MB0, MB1)
    s = lax.axis_index("seq")
    ch = lax.axis_index("chan")
    y, l, x = s // 16, (s // 4) % 4, s % 4
    sib = ch + 1 - 2 * (ch % 2)
    opp = (ch + 2) % 4
    h, c = ch // 2, ch % 2
    side = l // 2
    far = 2 * (1 - h)

    def seq_of(yy, ll, xx):
        return yy * 16 + ll * 4 + xx

    mirror = (seq_of(y, 3 - l, x), opp)
    x_plus, x_minus = (seq_of(y, l, (x + 1) % 4), ch), (seq_of(y, l, (x + 3) % 4), ch)
    y_plus, y_minus = (seq_of((y + 1) % 4, l, x), ch), (seq_of((y + 3) % 4, l, x), ch)

    bar = pltpu.get_barrier_semaphore()

    @pl.loop(1, 64, unroll=9)
    def _(k):
        pl.semaphore_signal(bar, inc=1, device_id=((s + k) % 64, ch), device_id_type=MESH)

    @pl.loop(1, 4, unroll=3)
    def _(k):
        pl.semaphore_signal(bar, inc=1, device_id=(s, (ch + k) % 4), device_id_type=MESH)

    pl.semaphore_signal(bar, inc=1, device_id=mirror, device_id_type=MESH)

    loads = [
        pltpu.make_async_copy(tok_in, X, ld.at[0]),
        pltpu.make_async_copy(upf_in, UR, ld.at[1]),
        pltpu.make_async_copy(dnf_in, DR, ld.at[2]),
        pltpu.make_async_copy(left_in, SL, ld.at[3]),
        pltpu.make_async_copy(right_in, SR, ld.at[4]),
        pltpu.make_async_copy(ups_in, US.at[ch, :, pl.ds(0, 96)], ld.at[5]),
        pltpu.make_async_copy(dns_in, DS.at[ch, :, pl.ds(0, 96)], ld.at[6]),
    ]
    for cp in loads:
        cp.start()

    eye = lax.broadcasted_iota(jnp.int32, (128, 128), 0) == lax.broadcasted_iota(jnp.int32, (128, 128), 1)
    loads[0].wait()

    @pl.loop(0, 16)
    def _(k):
        xb = X[k // 2, pl.ds(2 * (k % 2), 2)].reshape(128, W).astype(F32)
        col = jnp.sum(xb * xb, axis=1, keepdims=True)
        SQ[ch, pl.ds(k, 1), :] = jnp.sum(jnp.where(eye, col, 0.0), axis=0, keepdims=True)

    G[ch, 0] = jnp.broadcast_to(gseq_in[...].reshape(1, W), (16, W))
    G[ch, 1] = jnp.broadcast_to(gmlp_in[...].reshape(1, W), (16, W))
    pl.semaphore_wait(bar, 67)

    @pl.loop(1, 4)
    def _(k):
        to = (s, (ch + k) % 4)
        remote(SQ.at[ch], SQ.at[ch], sq_sem.at[0], sq_sem.at[1], to).start()
        remote(G.at[ch], G.at[ch], gm_sem.at[0], gm_sem.at[1], to).start()

    from_lane = lax.broadcasted_iota(jnp.int32, (W, 512), 0)
    to_lane = lax.broadcasted_iota(jnp.int32, (W, 512), 1)
    kept = ((to_lane & 127) < 96) & (from_lane == (to_lane >> 7) * 96 + (to_lane & 127))
    spread = kept.astype(F32).astype(BF16)
    loads[1].wait()
    loads[2].wait()

    @pl.loop(0, 3)
    def _(k):
        at = pl.ds(pl.multiple_of(k * 256, 256), 256)
        UF[ch, at, :] = dot(UR[at, :], spread).astype(BF16)

    @pl.loop(0, 6)
    def _(k):
        at = pl.ds(pl.multiple_of(k * 256, 256), 256)
        DF[ch, at, :] = dot(DR[at, :], spread).astype(BF16)

    ux = y * 4 + x
    uy = x * 4 + y

    def us_unit(blk, u, lanes=pl.ds(0, 1536)):
        return US.at[blk, u // 2, pl.ds(pl.multiple_of((u % 2) * 48, 16), 48), lanes]

    def us_row(blk, r, lanes=pl.ds(0, 1536)):
        return US.at[blk, pl.ds(r * 2, 2), pl.ds(0, 96), lanes]

    def uf_unit(blk, u, lanes=pl.ds(0, 512)):
        return UF.at[blk, pl.ds(pl.multiple_of(u * 48, 16), 48), lanes]

    def uf_row(blk, r, lanes=pl.ds(0, 512)):
        return UF.at[blk, pl.ds(pl.multiple_of(r * 192, 16), 192), lanes]

    def df_unit(blk, u, lanes=pl.ds(0, 512)):
        return DF.at[blk, pl.ds(pl.multiple_of(u * 96, 16), 96), lanes]

    def df_row(blk, r, lanes=pl.ds(0, 512)):
        return DF.at[blk, pl.ds(pl.multiple_of(r * 384, 16), 384), lanes]

    def ds_unit(blk, u, lanes=pl.ds(0, W)):
        return DS.at[blk, u, pl.ds(0, 96), lanes]

    first_unit = [
        remote(ups_in.at[ux // 2, pl.ds(pl.multiple_of((ux % 2) * 48, 16), 48)], us_unit(ch, ux), w1_send.at[0], w1_recv.at[0], mirror),
        remote(uf_unit(ch, uy), uf_unit(ch, uy), w1_send.at[1], w1_recv.at[1], mirror),
        remote(df_unit(ch, uy), df_unit(ch, uy), w1_send.at[2], w1_recv.at[2], mirror),
        remote(dns_in.at[x], ds_unit(ch, x), w1_send.at[3], w1_recv.at[3], mirror),
    ]
    for cp in first_unit:
        cp.start()

    tokens_across = [
        remote(X.at[pl.ds(2 * far, 4), pl.ds(2 * k, 2), 1 - side], XB.at[c], xb_sem.at[0], xb_sem.at[1], (s, far + k))
        for k in range(2)
    ]

    to_sib = (s, sib)
    own_block = [
        remote(ups_in, US.at[ch, :, pl.ds(0, 96)], sib_send.at[0], sib_recv.at[0], to_sib),
        remote(UF.at[ch], UF.at[ch], sib_send.at[1], sib_recv.at[1], to_sib),
        remote(DF.at[ch], DF.at[ch], sib_send.at[2], sib_recv.at[2], to_sib),
        remote(dns_in, DS.at[ch, :, pl.ds(0, 96)], sib_send.at[3], sib_recv.at[3], to_sib),
    ]
    other_block = [
        remote(US.at[opp, :, pl.ds(0, 96)], US.at[opp, :, pl.ds(0, 96)], sib_send.at[4], sib_recv.at[4], to_sib),
        remote(UF.at[opp], UF.at[opp], sib_send.at[5], sib_recv.at[5], to_sib),
        remote(DF.at[opp], DF.at[opp], sib_send.at[6], sib_recv.at[6], to_sib),
        remote(DS.at[opp, :, pl.ds(0, 96)], DS.at[opp, :, pl.ds(0, 96)], sib_send.at[7], sib_recv.at[7], to_sib),
    ]
    for cp in own_block:
        cp.start()

    xring, yring = (x, x_plus, x_minus), (y, y_plus, y_minus)
    ux_of = (lambda p: y * 4 + p, lambda p: p)
    uy_of = (lambda p: x * 4 + p, lambda p: p)
    tables = [
        (us_unit, us_row, 1536, xring, yring, ux_of),
        (uf_unit, uf_row, 512, yring, xring, uy_of),
        (df_unit, df_row, 512, yring, xring, uy_of),
        (ds_unit, None, 384, xring, None, (lambda p: p, None)),
    ]

    def ring_copies(stage, step):
        copies = []
        for j, (unit, row, width, ring_a, ring_b, (first, second)) in enumerate(tables):
            if stage and row is None:
                continue
            pos, plus, minus = (ring_a, ring_b)[stage]
            part, index = ((unit, first), (row, second))[stage]
            sem = ((j * 2 + stage) * 2 + step) * 2
            if step == 0:
                mine = part(opp, index(pos))
                copies += [
                    remote(mine, mine, wr_send.at[sem], wr_recv.at[sem], plus),
                    remote(mine, mine, wr_send.at[sem + 1], wr_recv.at[sem + 1], minus),
                ]
            else:
                half = width // 256 * 128
                below = part(opp, index((pos + 3) % 4), pl.ds(0, half))
                above = part(opp, index((pos + 1) % 4), pl.ds(half, width - half))
                copies += [
                    remote(below, below, wr_send.at[sem], wr_recv.at[sem], plus),
                    remote(above, above, wr_send.at[sem + 1], wr_recv.at[sem + 1], minus),
                ]
        return copies

    rings = [ring_copies(0, 0), ring_copies(0, 1), ring_copies(1, 0), ring_copies(1, 1)]

    US[:, :, pl.ds(96, 32), :] = jnp.zeros((4, 8, 32, 1536), BF16)
    DS[:, :, pl.ds(96, 32), :] = jnp.zeros((4, 4, 32, W), BF16)

    drain(SQ.at[pl.ds(0, 3)], sq_sem.at[1])
    scale = lax.rsqrt((SQ[0] + SQ[1] + SQ[2] + SQ[3]) / 1536.0 + EPS)
    RR[...] = scale
    loads[3].wait()
    gain = gseq_in[...].reshape(1, W).astype(F32)

    out_row = lax.broadcasted_iota(jnp.int32, (256, 256), 0)
    in_row = lax.broadcasted_iota(jnp.int32, (256, 256), 1)
    perm = (in_row == (out_row & 7) * 32 + (out_row >> 5) * 4 + ((out_row >> 3) & 3)).astype(F32).astype(BF16)

    def first(n):
        start, width = PARTS[n]
        cut = pl.ds(start, width)
        fs, s1, r1 = FS[n], S1[n], R1[n]

        @pl.loop(0, 8, unroll=4)
        def _(o):
            if n == 0:
                r = jnp.concatenate([RR[pl.ds(2 * o, 1), :], RR[pl.ds(2 * o + 1, 1), :]], axis=1)
                SL[o] = (SL[o].astype(F32) * r).astype(BF16)
            rows = X[o, :, :, :, cut].reshape(256, width)
            fs[o] = (dot(SL[o], rows) * gain[:, start : start + width]).astype(BF16)

        @pl.loop(0, 8)
        def _(k):
            g = (k + s // 8) % 8
            block = fs[:, pl.ds(pl.multiple_of(g * 32, 32), 32), :].reshape(256, width)
            s1[pl.ds(g * 8, 8)] = dot(perm, block).astype(BF16).reshape(8, 32, width)

            @pl.loop(0, 8, unroll=8)
            def _(j):
                d = g * 8 + (j + s) % 8

                @pl.when(d != s)
                def _():
                    remote(s1.at[d], r1.at[s], a1_sem.at[0, n], a1_sem.at[1, n], (d, ch)).start()

        r1[s] = s1[s]

    first(0)
    first(1)
    tokens_across[0].start()
    tokens_across[1].start()

    @pl.loop(0, 16)
    def _(k):
        col = jnp.sum(jnp.where(eye, RR[pl.ds(k, 1), :], 0.0), axis=1, keepdims=True)
        RC[k // 2, pl.ds(2 * (k % 2), 2)] = jnp.broadcast_to(col, (128, 128)).reshape(2, 2, 32, 128)

    for cp in first_unit:
        cp.wait_recv()
    for cp in rings[0]:
        cp.start()
    for k in range(3):
        for cp in rings[k]:
            cp.wait_recv()
        for cp in rings[k + 1]:
            cp.start()
    loads[4].wait()

    def second(n):
        width = PARTS[n][1]
        r1, gb, s2, r2, mb = R1[n], GB[n], S2[n], R2[n], MB[n]
        drain(r1.at[pl.ds(0, 63)], a1_sem.at[1, n])

        @pl.loop(0, 8, unroll=2)
        def _(g):
            part = r1[pl.ds(g * 8, 8)].astype(F32)
            for b in range(4):
                rows = part[:, 8 * b : 8 * b + 8, :].reshape(64, width)
                gb[b, pl.ds(pl.multiple_of(g * 64, 64), 64), :] = rows.astype(BF16)

        low = lax.broadcasted_iota(jnp.int32, (32, 8, width), 1) < 4

        @pl.loop(0, 2)
        def _(k):
            m = (k + y // 2) % 2
            halves = ([], [])
            for pair in range(2):
                even, odd = (
                    dot(SR[b, pl.ds(pl.multiple_of(m * 256, 256), 256), :], gb[b]).reshape(32, 8, width)
                    for b in (2 * pair, 2 * pair + 1)
                )
                halves[0].append(jnp.where(low, even, pltpu.roll(odd, 4, 1)))
                halves[1].append(jnp.where(low, pltpu.roll(even, 4, 1), odd))
            for half in range(2):
                s2[pl.ds(m * 32, 32), half] = jnp.concatenate(halves[half], axis=1).astype(BF16)

            @pl.loop(0, 32, unroll=8)
            def _(j):
                d = m * 32 + (j + s) % 32
                same = (d // 8) % 2 == side

                @pl.when(same & (d != s))
                def _():
                    remote(s2.at[d], r2.at[s], a2_sem.at[0, n], a2_sem.at[1, n], (d, ch)).start()

                @pl.when(jnp.logical_not(same))
                def _():
                    remote(s2.at[d, h], r2.at[s, h], a2_sem.at[0, n], a2_sem.at[1, n], (d, ch)).start()
                    remote(
                        s2.at[d, 1 - h], mb.at[c, y % 2, (l % 2) * 4 + x],
                        mb_sem.at[0, n], mb_sem.at[1, n], (d, far + y // 2),
                    ).start()

        r2[s] = s2[s]

    second(0)
    second(1)
    for cp in rings[3]:
        cp.wait_recv()
    for cp in other_block:
        cp.start()

    out_row = lax.broadcasted_iota(jnp.int32, (128, 128), 0)
    in_row = lax.broadcasted_iota(jnp.int32, (128, 128), 1)
    back = (in_row == ((out_row >> 2) & 7) * 16 + (out_row & 3) * 4 + (out_row >> 5)).astype(F32).astype(BF16)

    def streamed(xs, mixed, rc, gains):
        width = xs.shape[-1]
        xs = xs.reshape(128, width).astype(F32)
        rc = jnp.concatenate([rc.reshape(128, 128)] * (width // 128), axis=1)
        normed = (xs * rc * gains).astype(BF16).astype(F32)
        return (xs + dot(back, mixed.reshape(128, width)) * normed).astype(BF16).reshape(4, 32, width)

    def at_home(n, hh, yy, half):
        start, width = PARTS[n]
        o4, cut = pl.ds(4 * hh, 4), pl.ds(start, width)
        mixed = R2[n][pl.ds(yy * 16 + half * 8, 8), hh]
        ST[o4, yy, half, :, cut] = streamed(
            X[o4, yy, half, :, cut], mixed, RC[o4, yy, half], gain[:, start : start + width]
        )

    drain(R2[0].at[pl.ds(0, 47)], a2_sem.at[1, 0])

    @pl.loop(0, 4, unroll=2)
    def _(yy):
        at_home(0, 1 - h, yy, side)

    @pl.loop(0, 8, unroll=2)
    def _(g):
        at_home(0, h, g // 2, g % 2)

    drain(R2[1].at[pl.ds(0, 47)], a2_sem.at[1, 1])

    @pl.loop(0, 4, unroll=2)
    def _(yy):
        at_home(1, 1 - h, yy, side)

    for t in range(2):
        for k in range(2):
            remote(
                ST.at[pl.ds(2 * far + 2 * t, 2), pl.ds(2 * k, 2), side],
                TS.at[ch, pl.ds(2 * t, 2), :, side],
                st_sem.at[0, t], st_sem.at[1, t], (s, far + k),
            ).start()

    @pl.loop(0, 8, unroll=2)
    def _(g):
        at_home(1, h, g // 2, g % 2)

    for t in range(2):
        remote(
            ST.at[pl.ds(4 * h + 2 * t, 2), pl.ds(2 * (1 - c), 2)], TS.at[ch, pl.ds(2 * t, 2)],
            st_sem.at[0, t], st_sem.at[1, t], to_sib,
        ).start()
    TS[ch] = ST[pl.ds(4 * h, 4), pl.ds(2 * c, 2)]

    drain(G.at[pl.ds(0, 3)], gm_sem.at[1])
    drain(XB, xb_sem.at[1])
    for n, (start, width) in enumerate(PARTS):
        cut = pl.ds(start, width)
        drain(MB[n], mb_sem.at[1, n])
        for k in range(2):
            gains = G[far + k, 0, pl.ds(0, 1), cut].astype(F32)
            for yy in range(2):
                rc = RC[pl.ds(4 * h, 4), 2 * c + yy, 1 - side]
                TS[far + k, :, yy, 1 - side, :, cut] = streamed(XB[k, :, yy, :, cut], MB[n][k, yy], rc, gains)

    for cp in loads[5:]:
        cp.wait()
    for cp in own_block:
        cp.wait_recv()
    for cp in other_block:
        cp.wait_recv()

    def stream_of(i, at):
        return TS[i, at].reshape(256, W).astype(F32)

    @pl.loop(0, 2)
    def _(t):
        at = pl.ds(2 * t, 2)
        drain(TS.at[0], st_sem.at[1, t])
        squares = jnp.zeros((256, 1), F32)
        for i in range(4):
            v = stream_of(i, at)
            squares += jnp.sum(v * v, axis=1, keepdims=True)
        r2 = lax.rsqrt(squares / 1536.0 + EPS)
        projected = []
        for i in range(4):
            n = (stream_of(i, at) * r2 * G[i, 1, pl.ds(0, 1), :].astype(F32)).astype(BF16)
            projected.append([dot(n, UF[i, pl.ds(g * W, W), :]).astype(BF16) for g in range(2)])
        down = []
        for p in range(4):
            merged = [
                jnp.concatenate([projected[i][g][:, p * 128 : p * 128 + 128] for i in range(4)], axis=1) for g in range(2)
            ]
            acc = jnp.zeros((256, 512), F32)
            for n in range(3):
                lanes = pl.ds(n * 512, 512)
                gate, up = (dot(merged[g], US[p, pl.ds(g * 4, 4), :, lanes].reshape(512, 512)) for g in range(2))
                hidden = (gate / (1.0 + jnp.exp(-gate)) * up).astype(BF16)
                acc += dot(hidden, DF[p, pl.ds(n * 512, 512), :])
            down.append(acc.astype(BF16))
        for r in range(4):
            merged = jnp.concatenate([down[p][:, r * 128 : r * 128 + 128] for p in range(4)], axis=1)
            mlp = dot(merged, DS[r].reshape(512, W))
            OB[r, at] = (stream_of(r, at) + mlp).astype(BF16).reshape(2, 2, 2, 32, W)
        home = (pl.ds(4 * h + 2 * t, 2), pl.ds(2 * c, 2))
        for r in (far, far + 1, sib):
            remote(OB.at[r, at], out.at[home], out_send.at[t], out_recv.at[t], (s, r)).start()
        pltpu.make_async_copy(OB.at[ch, at], out.at[home], own_sem.at[t]).start()

    drain(SQ.at[pl.ds(0, 3)], sq_sem.at[0])
    drain(G.at[pl.ds(0, 3)], gm_sem.at[0])
    drain(XB, xb_sem.at[0])
    for n in range(2):
        drain(S1[n].at[pl.ds(0, 63)], a1_sem.at[0, n])
        drain(S2[n].at[pl.ds(0, 47)], a2_sem.at[0, n])
        drain(MB[n], mb_sem.at[0, n])
    for cp in first_unit + own_block + other_block + rings[0] + rings[1] + rings[2] + rings[3]:
        cp.wait_send()
    for t in range(2):
        drain(TS.at[0], st_sem.at[0, t])
        drain(out.at[pl.ds(0, 3)], out_send.at[t])
        drain(out.at[pl.ds(0, 3)], out_recv.at[t])
        drain(out.at[pl.ds(0, 1)], own_sem.at[t])


def on_device(
    tokens, norm_gain_seq, seq_left, seq_right, norm_gain_mlp, up_first, up_second, down_first, down_second
):
    rows = tokens.shape[0]
    hbm = pl.BlockSpec(memory_space=pl.ANY)
    vmem = pl.BlockSpec(memory_space=pltpu.VMEM)
    dma = pltpu.SemaphoreType.DMA
    out = pl.pallas_call(
        layer_kernel,
        out_shape=jax.ShapeDtypeStruct((8, 4, 2, 32, W), BF16),
        in_specs=[hbm, vmem, vmem] + [hbm] * 6,
        out_specs=hbm,
        scratch_shapes=[
            pltpu.VMEM((8, 4, 2, 32, W), BF16),
            pltpu.VMEM((4, 2, 16, W), BF16),
            pltpu.VMEM((8, 256, 256), BF16),
            pltpu.VMEM((4, 512, 512), BF16),
            pltpu.VMEM((4, 16, 128), F32),
            pltpu.VMEM((16, 128), F32),
            pltpu.VMEM((8, 4, 2, 32, 128), F32),
            *[pltpu.VMEM((8, 256, w), BF16) for _, w in PARTS],
            *[pltpu.VMEM((64, 32, w), BF16) for _, w in PARTS],
            *[pltpu.VMEM((64, 32, w), BF16) for _, w in PARTS],
            *[pltpu.VMEM((4, 512, w), BF16) for _, w in PARTS],
            *[pltpu.VMEM((64, 2, 16, w), BF16) for _, w in PARTS],
            *[pltpu.VMEM((64, 2, 16, w), BF16) for _, w in PARTS],
            *[pltpu.VMEM((2, 2, 8, 16, w), BF16) for _, w in PARTS],
            pltpu.VMEM((2, 4, 2, 32, W), BF16),
            pltpu.VMEM((8, 4, 2, 32, W), BF16),
            pltpu.VMEM((4, 4, 2, 2, 32, W), BF16),
            pltpu.VMEM((4, 4, 2, 2, 32, W), BF16),
            pltpu.VMEM((4, 768, 512), BF16),
            pltpu.VMEM((4, 8, 128, 1536), BF16),
            pltpu.VMEM((4, 1536, 512), BF16),
            pltpu.VMEM((4, 4, 128, W), BF16),
            pltpu.VMEM((768, W), BF16),
            pltpu.VMEM((1536, W), BF16),
            dma((7,)), dma((2,)), dma((2,)), dma((2,)), dma((2, 2)), dma((2, 2)), dma((2, 2)), dma((2, 2)), dma((2,)), dma((2,)), dma((2,)),
            dma((4,)), dma((4,)), dma((32,)), dma((32,)), dma((8,)), dma((8,)),
        ],
        compiler_params=pltpu.CompilerParams(
            collective_id=0, has_side_effects=True, vmem_limit_bytes=60 * 2**20
        ),
        name="layer",
    )(
        tokens.reshape(8, 4, 2, 32, W), norm_gain_seq, norm_gain_mlp, seq_left, seq_right, up_first.reshape(768, W),
        up_second.reshape(8, 96, 1536), down_first.reshape(1536, W), down_second.reshape(4, 96, W),
    )
    return out.reshape(rows, 1, W)


def solution(mesh):
    return jax.shard_map(
        on_device,
        mesh=mesh,
        in_specs=(
            P("seq", None, "chan"),
            P("chan"),
            P("seq", None, None),
            P("seq", None, None),
            P("chan"),
            P(None, "chan", None, None),
            P(None, "chan", None, None),
            P("chan", None, None),
            P("chan", None, None),
        ),
        out_specs=P("seq", None, "chan"),
        check_vma=False,
    )
```

```python
import jax
import jax.numpy as jnp
from jax import lax
from jax.experimental import pallas as pl
from jax.experimental.pallas import tpu as pltpu
from jax.sharding import PartitionSpec as P

MESH = pl.DeviceIdType.MESH
BF16 = jnp.bfloat16
F32 = jnp.float32
W = 384
EPS = 1e-6
PARTS = ((0, 256), (256, 128))


def dot(a, b):
    return jnp.dot(a, b, preferred_element_type=F32)


def remote(src, dst, send, recv, device):
    return pltpu.make_async_remote_copy(
        src_ref=src, dst_ref=dst, send_sem=send, recv_sem=recv, device_id=device, device_id_type=MESH
    )


def drain(ref, sem):
    pltpu.make_async_copy(ref, ref, sem).wait()


def layer_kernel(
    tok_in, gseq_in, gmlp_in, left_in, right_in, upf_in, ups_in, dnf_in, dns_in,
    out,
    X, G, SL, SR, SQ, RR, RC, FS0, FS1, S10, S11, R10, R11, GB0, GB1, S20, S21, R20, R21, MB0, MB1, XB, ST, TS, OB, UF, US, DF, DS, UR, DR,
    met, ld, sq_sem, gm_sem, xb_sem, a1_sem, a2_sem, mb_sem, st_sem, own_sem, out_send, out_recv, w1_send, w1_recv, wr_send, wr_recv, sib_send, sib_recv,
):
    FS, S1, R1, GB = (FS0, FS1), (S10, S11), (R10, R11), (GB0, GB1)
    S2, R2, MB = (S20, S21), (R20, R21), (MB0, MB1)
    s = lax.axis_index("seq")
    ch = lax.axis_index("chan")
    y, l, x = s // 16, (s // 4) % 4, s % 4
    sib = ch + 1 - 2 * (ch % 2)
    opp = (ch + 2) % 4
    h, c = ch // 2, ch % 2
    side = l // 2
    far = 2 * (1 - h)

    def seq_of(yy, ll, xx):
        return yy * 16 + ll * 4 + xx

    mirror = (seq_of(y, 3 - l, x), opp)
    x_plus, x_minus = (seq_of(y, l, (x + 1) % 4), ch), (seq_of(y, l, (x + 3) % 4), ch)
    y_plus, y_minus = (seq_of((y + 1) % 4, l, x), ch), (seq_of((y + 3) % 4, l, x), ch)

    bar = pltpu.get_barrier_semaphore()

    x_line = [(seq_of(y, l, (x + k) % 4), ch) for k in (1, 2, 3)]
    y_line = [(seq_of((y + k) % 4, l, x), ch) for k in (1, 2, 3)]
    z_line = [(seq_of(y, (l + k) % 4, x), ch) for k in (1, 2, 3)]

    def greet(sem, line):
        for to in line:
            pl.semaphore_signal(sem, inc=1, device_id=to, device_id_type=MESH)

    greet(bar, x_line + y_line + z_line)

    @pl.loop(1, 4, unroll=3)
    def _(k):
        pl.semaphore_signal(bar, inc=1, device_id=(s, (ch + k) % 4), device_id_type=MESH)

    pl.semaphore_signal(bar, inc=1, device_id=mirror, device_id_type=MESH)

    loads = [
        pltpu.make_async_copy(tok_in, X, ld.at[0]),
        pltpu.make_async_copy(upf_in, UR, ld.at[1]),
        pltpu.make_async_copy(dnf_in, DR, ld.at[2]),
        pltpu.make_async_copy(left_in, SL, ld.at[3]),
        pltpu.make_async_copy(right_in, SR, ld.at[4]),
        pltpu.make_async_copy(ups_in, US.at[ch, :, pl.ds(0, 96)], ld.at[5]),
        pltpu.make_async_copy(dns_in, DS.at[ch, :, pl.ds(0, 96)], ld.at[6]),
    ]
    for cp in loads:
        cp.start()

    eye = lax.broadcasted_iota(jnp.int32, (128, 128), 0) == lax.broadcasted_iota(jnp.int32, (128, 128), 1)
    loads[0].wait()

    @pl.loop(0, 16)
    def _(k):
        xb = X[k // 2, pl.ds(2 * (k % 2), 2)].reshape(128, W).astype(F32)
        col = jnp.sum(xb * xb, axis=1, keepdims=True)
        SQ[ch, pl.ds(k, 1), :] = jnp.sum(jnp.where(eye, col, 0.0), axis=0, keepdims=True)

    G[ch, 0] = jnp.broadcast_to(gseq_in[...].reshape(1, W), (16, W))
    G[ch, 1] = jnp.broadcast_to(gmlp_in[...].reshape(1, W), (16, W))
    pl.semaphore_wait(bar, 13)

    @pl.loop(1, 4)
    def _(k):
        to = (s, (ch + k) % 4)
        remote(SQ.at[ch], SQ.at[ch], sq_sem.at[0], sq_sem.at[1], to).start()
        remote(G.at[ch], G.at[ch], gm_sem.at[0], gm_sem.at[1], to).start()

    greet(met.at[0], y_line)

    from_lane = lax.broadcasted_iota(jnp.int32, (W, 512), 0)
    to_lane = lax.broadcasted_iota(jnp.int32, (W, 512), 1)
    kept = ((to_lane & 127) < 96) & (from_lane == (to_lane >> 7) * 96 + (to_lane & 127))
    spread = kept.astype(F32).astype(BF16)
    loads[1].wait()
    loads[2].wait()

    @pl.loop(0, 3)
    def _(k):
        at = pl.ds(pl.multiple_of(k * 256, 256), 256)
        UF[ch, at, :] = dot(UR[at, :], spread).astype(BF16)

    @pl.loop(0, 6)
    def _(k):
        at = pl.ds(pl.multiple_of(k * 256, 256), 256)
        DF[ch, at, :] = dot(DR[at, :], spread).astype(BF16)

    pl.semaphore_wait(met.at[0], 3)
    greet(met.at[1], z_line)

    ux = y * 4 + x
    uy = x * 4 + y

    def us_unit(blk, u, lanes=pl.ds(0, 1536)):
        return US.at[blk, u // 2, pl.ds(pl.multiple_of((u % 2) * 48, 16), 48), lanes]

    def us_row(blk, r, lanes=pl.ds(0, 1536)):
        return US.at[blk, pl.ds(r * 2, 2), pl.ds(0, 96), lanes]

    def uf_unit(blk, u, lanes=pl.ds(0, 512)):
        return UF.at[blk, pl.ds(pl.multiple_of(u * 48, 16), 48), lanes]

    def uf_row(blk, r, lanes=pl.ds(0, 512)):
        return UF.at[blk, pl.ds(pl.multiple_of(r * 192, 16), 192), lanes]

    def df_unit(blk, u, lanes=pl.ds(0, 512)):
        return DF.at[blk, pl.ds(pl.multiple_of(u * 96, 16), 96), lanes]

    def df_row(blk, r, lanes=pl.ds(0, 512)):
        return DF.at[blk, pl.ds(pl.multiple_of(r * 384, 16), 384), lanes]

    def ds_unit(blk, u, lanes=pl.ds(0, W)):
        return DS.at[blk, u, pl.ds(0, 96), lanes]

    first_unit = [
        remote(ups_in.at[ux // 2, pl.ds(pl.multiple_of((ux % 2) * 48, 16), 48)], us_unit(ch, ux), w1_send.at[0], w1_recv.at[0], mirror),
        remote(uf_unit(ch, uy), uf_unit(ch, uy), w1_send.at[1], w1_recv.at[1], mirror),
        remote(df_unit(ch, uy), df_unit(ch, uy), w1_send.at[2], w1_recv.at[2], mirror),
        remote(dns_in.at[x], ds_unit(ch, x), w1_send.at[3], w1_recv.at[3], mirror),
    ]
    for cp in first_unit:
        cp.start()

    tokens_across = [
        remote(X.at[pl.ds(2 * far, 4), pl.ds(2 * k, 2), 1 - side], XB.at[c], xb_sem.at[0], xb_sem.at[1], (s, far + k))
        for k in range(2)
    ]

    to_sib = (s, sib)
    own_block = [
        remote(ups_in, US.at[ch, :, pl.ds(0, 96)], sib_send.at[0], sib_recv.at[0], to_sib),
        remote(UF.at[ch], UF.at[ch], sib_send.at[1], sib_recv.at[1], to_sib),
        remote(DF.at[ch], DF.at[ch], sib_send.at[2], sib_recv.at[2], to_sib),
        remote(dns_in, DS.at[ch, :, pl.ds(0, 96)], sib_send.at[3], sib_recv.at[3], to_sib),
    ]
    other_block = [
        remote(US.at[opp, :, pl.ds(0, 96)], US.at[opp, :, pl.ds(0, 96)], sib_send.at[4], sib_recv.at[4], to_sib),
        remote(UF.at[opp], UF.at[opp], sib_send.at[5], sib_recv.at[5], to_sib),
        remote(DF.at[opp], DF.at[opp], sib_send.at[6], sib_recv.at[6], to_sib),
        remote(DS.at[opp, :, pl.ds(0, 96)], DS.at[opp, :, pl.ds(0, 96)], sib_send.at[7], sib_recv.at[7], to_sib),
    ]
    for cp in own_block:
        cp.start()

    xring, yring = (x, x_plus, x_minus), (y, y_plus, y_minus)
    ux_of = (lambda p: y * 4 + p, lambda p: p)
    uy_of = (lambda p: x * 4 + p, lambda p: p)
    tables = [
        (us_unit, us_row, 1536, xring, yring, ux_of),
        (uf_unit, uf_row, 512, yring, xring, uy_of),
        (df_unit, df_row, 512, yring, xring, uy_of),
        (ds_unit, None, 384, xring, None, (lambda p: p, None)),
    ]

    def ring_copies(stage, step):
        copies = []
        for j, (unit, row, width, ring_a, ring_b, (first, second)) in enumerate(tables):
            if stage and row is None:
                continue
            pos, plus, minus = (ring_a, ring_b)[stage]
            part, index = ((unit, first), (row, second))[stage]
            sem = ((j * 2 + stage) * 2 + step) * 2
            if step == 0:
                mine = part(opp, index(pos))
                copies += [
                    remote(mine, mine, wr_send.at[sem], wr_recv.at[sem], plus),
                    remote(mine, mine, wr_send.at[sem + 1], wr_recv.at[sem + 1], minus),
                ]
            else:
                half = width // 256 * 128
                below = part(opp, index((pos + 3) % 4), pl.ds(0, half))
                above = part(opp, index((pos + 1) % 4), pl.ds(half, width - half))
                copies += [
                    remote(below, below, wr_send.at[sem], wr_recv.at[sem], plus),
                    remote(above, above, wr_send.at[sem + 1], wr_recv.at[sem + 1], minus),
                ]
        return copies

    rings = [ring_copies(0, 0), ring_copies(0, 1), ring_copies(1, 0), ring_copies(1, 1)]

    US[:, :, pl.ds(96, 32), :] = jnp.zeros((4, 8, 32, 1536), BF16)
    DS[:, :, pl.ds(96, 32), :] = jnp.zeros((4, 4, 32, W), BF16)

    drain(SQ.at[pl.ds(0, 3)], sq_sem.at[1])
    scale = lax.rsqrt((SQ[0] + SQ[1] + SQ[2] + SQ[3]) / 1536.0 + EPS)
    RR[...] = scale
    loads[3].wait()
    gain = gseq_in[...].reshape(1, W).astype(F32)

    out_row = lax.broadcasted_iota(jnp.int32, (256, 256), 0)
    in_row = lax.broadcasted_iota(jnp.int32, (256, 256), 1)
    perm = (in_row == (out_row & 7) * 32 + (out_row >> 5) * 4 + ((out_row >> 3) & 3)).astype(F32).astype(BF16)

    def first(n):
        start, width = PARTS[n]
        cut = pl.ds(start, width)
        fs, s1, r1 = FS[n], S1[n], R1[n]

        @pl.loop(0, 8, unroll=4)
        def _(o):
            if n == 0:
                r = jnp.concatenate([RR[pl.ds(2 * o, 1), :], RR[pl.ds(2 * o + 1, 1), :]], axis=1)
                SL[o] = (SL[o].astype(F32) * r).astype(BF16)
            rows = X[o, :, :, :, cut].reshape(256, width)
            fs[o] = (dot(SL[o], rows) * gain[:, start : start + width]).astype(BF16)

        @pl.loop(0, 8)
        def _(k):
            g = (k + s // 8) % 8
            block = fs[:, pl.ds(pl.multiple_of(g * 32, 32), 32), :].reshape(256, width)
            s1[pl.ds(g * 8, 8)] = dot(perm, block).astype(BF16).reshape(8, 32, width)

            @pl.loop(0, 8, unroll=8)
            def _(j):
                d = g * 8 + (j + s) % 8

                @pl.when(d != s)
                def _():
                    remote(s1.at[d], r1.at[s], a1_sem.at[0, n], a1_sem.at[1, n], (d, ch)).start()

        r1[s] = s1[s]

    pl.semaphore_wait(met.at[1], 3)
    first(0)
    first(1)
    tokens_across[0].start()
    tokens_across[1].start()

    @pl.loop(0, 16)
    def _(k):
        col = jnp.sum(jnp.where(eye, RR[pl.ds(k, 1), :], 0.0), axis=1, keepdims=True)
        RC[k // 2, pl.ds(2 * (k % 2), 2)] = jnp.broadcast_to(col, (128, 128)).reshape(2, 2, 32, 128)

    for cp in first_unit:
        cp.wait_recv()
    for cp in rings[0]:
        cp.start()
    for cp in rings[0]:
        cp.wait_recv()
    for cp in rings[1]:
        cp.start()
    loads[4].wait()

    def second(n):
        width = PARTS[n][1]
        r1, gb, s2, r2, mb = R1[n], GB[n], S2[n], R2[n], MB[n]
        drain(r1.at[pl.ds(0, 63)], a1_sem.at[1, n])

        @pl.loop(0, 8, unroll=2)
        def _(g):
            part = r1[pl.ds(g * 8, 8)].astype(F32)
            for b in range(4):
                rows = part[:, 8 * b : 8 * b + 8, :].reshape(64, width)
                gb[b, pl.ds(pl.multiple_of(g * 64, 64), 64), :] = rows.astype(BF16)

        low = lax.broadcasted_iota(jnp.int32, (32, 8, width), 1) < 4

        @pl.loop(0, 2)
        def _(k):
            m = (k + y // 2) % 2
            halves = ([], [])
            for pair in range(2):
                even, odd = (
                    dot(SR[b, pl.ds(pl.multiple_of(m * 256, 256), 256), :], gb[b]).reshape(32, 8, width)
                    for b in (2 * pair, 2 * pair + 1)
                )
                halves[0].append(jnp.where(low, even, pltpu.roll(odd, 4, 1)))
                halves[1].append(jnp.where(low, pltpu.roll(even, 4, 1), odd))
            for half in range(2):
                s2[pl.ds(m * 32, 32), half] = jnp.concatenate(halves[half], axis=1).astype(BF16)

            @pl.loop(0, 32, unroll=8)
            def _(j):
                d = m * 32 + (j + s) % 32
                same = (d // 8) % 2 == side

                @pl.when(same & (d != s))
                def _():
                    remote(s2.at[d], r2.at[s], a2_sem.at[0, n], a2_sem.at[1, n], (d, ch)).start()

                @pl.when(jnp.logical_not(same))
                def _():
                    remote(s2.at[d, h], r2.at[s, h], a2_sem.at[0, n], a2_sem.at[1, n], (d, ch)).start()
                    remote(
                        s2.at[d, 1 - h], mb.at[c, y % 2, (l % 2) * 4 + x],
                        mb_sem.at[0, n], mb_sem.at[1, n], (d, far + y // 2),
                    ).start()

        r2[s] = s2[s]

    second(0)
    for cp in rings[1]:
        cp.wait_recv()
    for cp in rings[2]:
        cp.start()
    second(1)
    for cp in rings[2]:
        cp.wait_recv()
    for cp in rings[3]:
        cp.start()

    out_row = lax.broadcasted_iota(jnp.int32, (128, 128), 0)
    in_row = lax.broadcasted_iota(jnp.int32, (128, 128), 1)
    back = (in_row == ((out_row >> 2) & 7) * 16 + (out_row & 3) * 4 + (out_row >> 5)).astype(F32).astype(BF16)

    def streamed(xs, mixed, rc, gains):
        width = xs.shape[-1]
        xs = xs.reshape(128, width).astype(F32)
        rc = jnp.concatenate([rc.reshape(128, 128)] * (width // 128), axis=1)
        normed = (xs * rc * gains).astype(BF16).astype(F32)
        return (xs + dot(back, mixed.reshape(128, width)) * normed).astype(BF16).reshape(4, 32, width)

    def at_home(n, hh, yy, half):
        start, width = PARTS[n]
        o4, cut = pl.ds(4 * hh, 4), pl.ds(start, width)
        mixed = R2[n][pl.ds(yy * 16 + half * 8, 8), hh]
        ST[o4, yy, half, :, cut] = streamed(
            X[o4, yy, half, :, cut], mixed, RC[o4, yy, half], gain[:, start : start + width]
        )

    drain(R2[0].at[pl.ds(0, 47)], a2_sem.at[1, 0])

    @pl.loop(0, 4, unroll=2)
    def _(yy):
        at_home(0, 1 - h, yy, side)

    @pl.loop(0, 8, unroll=2)
    def _(g):
        at_home(0, h, g // 2, g % 2)

    for cp in rings[3]:
        cp.wait_recv()
    for cp in other_block:
        cp.start()
    drain(R2[1].at[pl.ds(0, 47)], a2_sem.at[1, 1])

    @pl.loop(0, 4, unroll=2)
    def _(yy):
        at_home(1, 1 - h, yy, side)

    for t in range(2):
        for k in range(2):
            remote(
                ST.at[pl.ds(2 * far + 2 * t, 2), pl.ds(2 * k, 2), side],
                TS.at[ch, pl.ds(2 * t, 2), :, side],
                st_sem.at[0, t], st_sem.at[1, t], (s, far + k),
            ).start()

    @pl.loop(0, 8, unroll=2)
    def _(g):
        at_home(1, h, g // 2, g % 2)

    for t in range(2):
        remote(
            ST.at[pl.ds(4 * h + 2 * t, 2), pl.ds(2 * (1 - c), 2)], TS.at[ch, pl.ds(2 * t, 2)],
            st_sem.at[0, t], st_sem.at[1, t], to_sib,
        ).start()
    TS[ch] = ST[pl.ds(4 * h, 4), pl.ds(2 * c, 2)]

    drain(G.at[pl.ds(0, 3)], gm_sem.at[1])
    drain(XB, xb_sem.at[1])
    for n, (start, width) in enumerate(PARTS):
        cut = pl.ds(start, width)
        drain(MB[n], mb_sem.at[1, n])
        for k in range(2):
            gains = G[far + k, 0, pl.ds(0, 1), cut].astype(F32)
            for yy in range(2):
                rc = RC[pl.ds(4 * h, 4), 2 * c + yy, 1 - side]
                TS[far + k, :, yy, 1 - side, :, cut] = streamed(XB[k, :, yy, :, cut], MB[n][k, yy], rc, gains)

    for cp in loads[5:]:
        cp.wait()
    for cp in own_block:
        cp.wait_recv()
    for cp in other_block:
        cp.wait_recv()

    def stream_of(i, at):
        return TS[i, at].reshape(256, W).astype(F32)

    @pl.loop(0, 2)
    def _(t):
        at = pl.ds(2 * t, 2)
        drain(TS.at[0], st_sem.at[1, t])
        squares = jnp.zeros((256, 1), F32)
        for i in range(4):
            v = stream_of(i, at)
            squares += jnp.sum(v * v, axis=1, keepdims=True)
        r2 = lax.rsqrt(squares / 1536.0 + EPS)
        projected = []
        for i in range(4):
            n = (stream_of(i, at) * r2 * G[i, 1, pl.ds(0, 1), :].astype(F32)).astype(BF16)
            projected.append([dot(n, UF[i, pl.ds(g * W, W), :]).astype(BF16) for g in range(2)])
        down = []
        for p in range(4):
            merged = [
                jnp.concatenate([projected[i][g][:, p * 128 : p * 128 + 128] for i in range(4)], axis=1) for g in range(2)
            ]
            acc = jnp.zeros((256, 512), F32)
            for n in range(3):
                lanes = pl.ds(n * 512, 512)
                gate, up = (dot(merged[g], US[p, pl.ds(g * 4, 4), :, lanes].reshape(512, 512)) for g in range(2))
                hidden = (gate / (1.0 + jnp.exp(-gate)) * up).astype(BF16)
                acc += dot(hidden, DF[p, pl.ds(n * 512, 512), :])
            down.append(acc.astype(BF16))
        for r in range(4):
            merged = jnp.concatenate([down[p][:, r * 128 : r * 128 + 128] for p in range(4)], axis=1)
            mlp = dot(merged, DS[r].reshape(512, W))
            OB[r, at] = (stream_of(r, at) + mlp).astype(BF16).reshape(2, 2, 2, 32, W)
        home = (pl.ds(4 * h + 2 * t, 2), pl.ds(2 * c, 2))
        for r in (far, far + 1, sib):
            remote(OB.at[r, at], out.at[home], out_send.at[t], out_recv.at[t], (s, r)).start()
        pltpu.make_async_copy(OB.at[ch, at], out.at[home], own_sem.at[t]).start()

    drain(SQ.at[pl.ds(0, 3)], sq_sem.at[0])
    drain(G.at[pl.ds(0, 3)], gm_sem.at[0])
    drain(XB, xb_sem.at[0])
    for n in range(2):
        drain(S1[n].at[pl.ds(0, 63)], a1_sem.at[0, n])
        drain(S2[n].at[pl.ds(0, 47)], a2_sem.at[0, n])
        drain(MB[n], mb_sem.at[0, n])
    for cp in first_unit + own_block + other_block + rings[0] + rings[1] + rings[2] + rings[3]:
        cp.wait_send()
    for t in range(2):
        drain(TS.at[0], st_sem.at[0, t])
        drain(out.at[pl.ds(0, 3)], out_send.at[t])
        drain(out.at[pl.ds(0, 3)], out_recv.at[t])
        drain(out.at[pl.ds(0, 1)], own_sem.at[t])


def on_device(
    tokens, norm_gain_seq, seq_left, seq_right, norm_gain_mlp, up_first, up_second, down_first, down_second
):
    rows = tokens.shape[0]
    hbm = pl.BlockSpec(memory_space=pl.ANY)
    vmem = pl.BlockSpec(memory_space=pltpu.VMEM)
    dma = pltpu.SemaphoreType.DMA
    out = pl.pallas_call(
        layer_kernel,
        out_shape=jax.ShapeDtypeStruct((8, 4, 2, 32, W), BF16),
        in_specs=[hbm, vmem, vmem] + [hbm] * 6,
        out_specs=hbm,
        scratch_shapes=[
            pltpu.VMEM((8, 4, 2, 32, W), BF16),
            pltpu.VMEM((4, 2, 16, W), BF16),
            pltpu.VMEM((8, 256, 256), BF16),
            pltpu.VMEM((4, 512, 512), BF16),
            pltpu.VMEM((4, 16, 128), F32),
            pltpu.VMEM((16, 128), F32),
            pltpu.VMEM((8, 4, 2, 32, 128), F32),
            *[pltpu.VMEM((8, 256, w), BF16) for _, w in PARTS],
            *[pltpu.VMEM((64, 32, w), BF16) for _, w in PARTS],
            *[pltpu.VMEM((64, 32, w), BF16) for _, w in PARTS],
            *[pltpu.VMEM((4, 512, w), BF16) for _, w in PARTS],
            *[pltpu.VMEM((64, 2, 16, w), BF16) for _, w in PARTS],
            *[pltpu.VMEM((64, 2, 16, w), BF16) for _, w in PARTS],
            *[pltpu.VMEM((2, 2, 8, 16, w), BF16) for _, w in PARTS],
            pltpu.VMEM((2, 4, 2, 32, W), BF16),
            pltpu.VMEM((8, 4, 2, 32, W), BF16),
            pltpu.VMEM((4, 4, 2, 2, 32, W), BF16),
            pltpu.VMEM((4, 4, 2, 2, 32, W), BF16),
            pltpu.VMEM((4, 768, 512), BF16),
            pltpu.VMEM((4, 8, 128, 1536), BF16),
            pltpu.VMEM((4, 1536, 512), BF16),
            pltpu.VMEM((4, 4, 128, W), BF16),
            pltpu.VMEM((768, W), BF16),
            pltpu.VMEM((1536, W), BF16),
            pltpu.SemaphoreType.REGULAR((2,)),
            dma((7,)), dma((2,)), dma((2,)), dma((2,)), dma((2, 2)), dma((2, 2)), dma((2, 2)), dma((2, 2)), dma((2,)), dma((2,)), dma((2,)),
            dma((4,)), dma((4,)), dma((32,)), dma((32,)), dma((8,)), dma((8,)),
        ],
        compiler_params=pltpu.CompilerParams(
            collective_id=0, has_side_effects=True, vmem_limit_bytes=60 * 2**20
        ),
        name="layer",
    )(
        tokens.reshape(8, 4, 2, 32, W), norm_gain_seq, norm_gain_mlp, seq_left, seq_right, up_first.reshape(768, W),
        up_second.reshape(8, 96, 1536), down_first.reshape(1536, W), down_second.reshape(4, 96, W),
    )
    return out.reshape(rows, 1, W)


def solution(mesh):
    return jax.shard_map(
        on_device,
        mesh=mesh,
        in_specs=(
            P("seq", None, "chan"),
            P("chan"),
            P("seq", None, None),
            P("seq", None, None),
            P("chan"),
            P(None, "chan", None, None),
            P(None, "chan", None, None),
            P("chan", None, None),
            P("chan", None, None),
        ),
        out_specs=P("seq", None, "chan"),
        check_vma=False,
    )
```

```python
import jax
import jax.numpy as jnp
from jax import lax
from jax.experimental import pallas as pl
from jax.experimental.pallas import tpu as pltpu
from jax.sharding import PartitionSpec as P

MESH = pl.DeviceIdType.MESH
BF16 = jnp.bfloat16
F32 = jnp.float32
W = 384
EPS = 1e-6
PARTS = ((0, 256), (256, 128))


def dot(a, b):
    return jnp.dot(a, b, preferred_element_type=F32)


def remote(src, dst, send, recv, device):
    return pltpu.make_async_remote_copy(
        src_ref=src, dst_ref=dst, send_sem=send, recv_sem=recv, device_id=device, device_id_type=MESH
    )


def drain(ref, sem):
    pltpu.make_async_copy(ref, ref, sem).wait()


def layer_kernel(
    tok_in, gseq_in, gmlp_in, left_in, right_in, upf_in, ups_in, dnf_in, dns_in,
    out,
    X, G, SL, SR, SQ, RR, RC, FS0, FS1, S10, S11, R10, R11, GB0, GB1, S20, S21, R20, R21, MB0, MB1, XB, ST, TS, OB, UF, US, DF, DS, UR, DR,
    met, ld, sq_sem, gm_sem, xb_sem, a1_sem, a2_sem, mb_sem, st_sem, own_sem, out_send, out_recv, w1_send, w1_recv, wr_send, wr_recv, sib_send, sib_recv,
):
    FS, S1, R1, GB = (FS0, FS1), (S10, S11), (R10, R11), (GB0, GB1)
    S2, R2, MB = (S20, S21), (R20, R21), (MB0, MB1)
    s = lax.axis_index("seq")
    ch = lax.axis_index("chan")
    y, l, x = s // 16, (s // 4) % 4, s % 4
    sib = ch + 1 - 2 * (ch % 2)
    opp = (ch + 2) % 4
    h, c = ch // 2, ch % 2
    side = l // 2
    far = 2 * (1 - h)

    def seq_of(yy, ll, xx):
        return yy * 16 + ll * 4 + xx

    mirror = (seq_of(y, 3 - l, x), opp)
    x_plus, x_minus = (seq_of(y, l, (x + 1) % 4), ch), (seq_of(y, l, (x + 3) % 4), ch)
    y_plus, y_minus = (seq_of((y + 1) % 4, l, x), ch), (seq_of((y + 3) % 4, l, x), ch)

    bar = pltpu.get_barrier_semaphore()

    x_line = [(seq_of(y, l, (x + k) % 4), ch) for k in (1, 2, 3)]
    y_line = [(seq_of((y + k) % 4, l, x), ch) for k in (1, 2, 3)]
    z_line = [(seq_of(y, (l + k) % 4, x), ch) for k in (1, 2, 3)]

    def greet(sem, line):
        for to in line:
            pl.semaphore_signal(sem, inc=1, device_id=to, device_id_type=MESH)

    greet(bar, x_line + y_line + z_line)

    @pl.loop(1, 4, unroll=3)
    def _(k):
        pl.semaphore_signal(bar, inc=1, device_id=(s, (ch + k) % 4), device_id_type=MESH)

    pl.semaphore_signal(bar, inc=1, device_id=mirror, device_id_type=MESH)

    loads = [
        pltpu.make_async_copy(tok_in, X, ld.at[0]),
        pltpu.make_async_copy(upf_in, UR, ld.at[1]),
        pltpu.make_async_copy(dnf_in, DR, ld.at[2]),
        pltpu.make_async_copy(left_in, SL, ld.at[3]),
        pltpu.make_async_copy(right_in, SR, ld.at[4]),
        pltpu.make_async_copy(ups_in, US.at[ch, :, pl.ds(0, 96)], ld.at[5]),
        pltpu.make_async_copy(dns_in, DS.at[ch, :, pl.ds(0, 96)], ld.at[6]),
    ]
    for cp in loads:
        cp.start()

    eye = lax.broadcasted_iota(jnp.int32, (128, 128), 0) == lax.broadcasted_iota(jnp.int32, (128, 128), 1)
    loads[0].wait()

    @pl.loop(0, 16)
    def _(k):
        xb = X[k // 2, pl.ds(2 * (k % 2), 2)].reshape(128, W).astype(F32)
        col = jnp.sum(xb * xb, axis=1, keepdims=True)
        SQ[ch, pl.ds(k, 1), :] = jnp.sum(jnp.where(eye, col, 0.0), axis=0, keepdims=True)

    G[ch, 0] = jnp.broadcast_to(gseq_in[...].reshape(1, W), (16, W))
    G[ch, 1] = jnp.broadcast_to(gmlp_in[...].reshape(1, W), (16, W))
    pl.semaphore_wait(bar, 13)

    @pl.loop(1, 4)
    def _(k):
        to = (s, (ch + k) % 4)
        remote(SQ.at[ch], SQ.at[ch], sq_sem.at[0], sq_sem.at[1], to).start()
        remote(G.at[ch], G.at[ch], gm_sem.at[0], gm_sem.at[1], to).start()

    greet(met.at[0], y_line)

    from_lane = lax.broadcasted_iota(jnp.int32, (W, 512), 0)
    to_lane = lax.broadcasted_iota(jnp.int32, (W, 512), 1)
    kept = ((to_lane & 127) < 96) & (from_lane == (to_lane >> 7) * 96 + (to_lane & 127))
    spread = kept.astype(F32).astype(BF16)
    loads[1].wait()
    loads[2].wait()

    @pl.loop(0, 3)
    def _(k):
        at = pl.ds(pl.multiple_of(k * 256, 256), 256)
        UF[ch, at, :] = dot(UR[at, :], spread).astype(BF16)

    @pl.loop(0, 6)
    def _(k):
        at = pl.ds(pl.multiple_of(k * 256, 256), 256)
        DF[ch, at, :] = dot(DR[at, :], spread).astype(BF16)

    pl.semaphore_wait(met.at[0], 3)
    greet(met.at[1], z_line)

    ux = y * 4 + x
    uy = x * 4 + y

    def us_unit(blk, u, lanes=pl.ds(0, 1536)):
        return US.at[blk, u // 2, pl.ds(pl.multiple_of((u % 2) * 48, 16), 48), lanes]

    def us_row(blk, r, lanes=pl.ds(0, 1536)):
        return US.at[blk, pl.ds(r * 2, 2), pl.ds(0, 96), lanes]

    def uf_unit(blk, u, lanes=pl.ds(0, 512)):
        return UF.at[blk, pl.ds(pl.multiple_of(u * 48, 16), 48), lanes]

    def uf_row(blk, r, lanes=pl.ds(0, 512)):
        return UF.at[blk, pl.ds(pl.multiple_of(r * 192, 16), 192), lanes]

    def df_unit(blk, u, lanes=pl.ds(0, 512)):
        return DF.at[blk, pl.ds(pl.multiple_of(u * 96, 16), 96), lanes]

    def df_row(blk, r, lanes=pl.ds(0, 512)):
        return DF.at[blk, pl.ds(pl.multiple_of(r * 384, 16), 384), lanes]

    def ds_unit(blk, u, lanes=pl.ds(0, W)):
        return DS.at[blk, u, pl.ds(0, 96), lanes]

    first_unit = [
        remote(ups_in.at[ux // 2, pl.ds(pl.multiple_of((ux % 2) * 48, 16), 48)], us_unit(ch, ux), w1_send.at[0], w1_recv.at[0], mirror),
        remote(uf_unit(ch, uy), uf_unit(ch, uy), w1_send.at[1], w1_recv.at[1], mirror),
        remote(df_unit(ch, uy), df_unit(ch, uy), w1_send.at[2], w1_recv.at[2], mirror),
        remote(dns_in.at[x], ds_unit(ch, x), w1_send.at[3], w1_recv.at[3], mirror),
    ]
    for cp in first_unit:
        cp.start()

    tokens_across = [
        remote(X.at[pl.ds(2 * far, 4), pl.ds(2 * k, 2), 1 - side], XB.at[c], xb_sem.at[0], xb_sem.at[1], (s, far + k))
        for k in range(2)
    ]

    to_sib = (s, sib)
    own_block = [
        remote(ups_in, US.at[ch, :, pl.ds(0, 96)], sib_send.at[0], sib_recv.at[0], to_sib),
        remote(UF.at[ch], UF.at[ch], sib_send.at[1], sib_recv.at[1], to_sib),
        remote(DF.at[ch], DF.at[ch], sib_send.at[2], sib_recv.at[2], to_sib),
        remote(dns_in, DS.at[ch, :, pl.ds(0, 96)], sib_send.at[3], sib_recv.at[3], to_sib),
    ]
    other_block = [
        remote(US.at[opp, :, pl.ds(0, 96)], US.at[opp, :, pl.ds(0, 96)], sib_send.at[4], sib_recv.at[4], to_sib),
        remote(UF.at[opp], UF.at[opp], sib_send.at[5], sib_recv.at[5], to_sib),
        remote(DF.at[opp], DF.at[opp], sib_send.at[6], sib_recv.at[6], to_sib),
        remote(DS.at[opp, :, pl.ds(0, 96)], DS.at[opp, :, pl.ds(0, 96)], sib_send.at[7], sib_recv.at[7], to_sib),
    ]
    for cp in own_block:
        cp.start()

    xring, yring = (x, x_plus, x_minus), (y, y_plus, y_minus)
    ux_of = (lambda p: y * 4 + p, lambda p: p)
    uy_of = (lambda p: x * 4 + p, lambda p: p)
    tables = [
        (us_unit, us_row, 1536, xring, yring, ux_of),
        (uf_unit, uf_row, 512, yring, xring, uy_of),
        (df_unit, df_row, 512, yring, xring, uy_of),
        (ds_unit, None, 384, xring, None, (lambda p: p, None)),
    ]

    def ring_copies(stage, step):
        copies = []
        for j, (unit, row, width, ring_a, ring_b, (first, second)) in enumerate(tables):
            if stage and row is None:
                continue
            pos, plus, minus = (ring_a, ring_b)[stage]
            part, index = ((unit, first), (row, second))[stage]
            sem = ((j * 2 + stage) * 2 + step) * 2
            if step == 0:
                mine = part(opp, index(pos))
                copies += [
                    remote(mine, mine, wr_send.at[sem], wr_recv.at[sem], plus),
                    remote(mine, mine, wr_send.at[sem + 1], wr_recv.at[sem + 1], minus),
                ]
            else:
                half = width // 256 * 128
                below = part(opp, index((pos + 3) % 4), pl.ds(0, half))
                above = part(opp, index((pos + 1) % 4), pl.ds(half, width - half))
                copies += [
                    remote(below, below, wr_send.at[sem], wr_recv.at[sem], plus),
                    remote(above, above, wr_send.at[sem + 1], wr_recv.at[sem + 1], minus),
                ]
        return copies

    rings = [ring_copies(0, 0), ring_copies(0, 1), ring_copies(1, 0), ring_copies(1, 1)]

    US[:, :, pl.ds(96, 32), :] = jnp.zeros((4, 8, 32, 1536), BF16)
    DS[:, :, pl.ds(96, 32), :] = jnp.zeros((4, 4, 32, W), BF16)

    drain(SQ.at[pl.ds(0, 3)], sq_sem.at[1])
    scale = lax.rsqrt((SQ[0] + SQ[1] + SQ[2] + SQ[3]) / 1536.0 + EPS)
    RR[...] = scale
    loads[3].wait()
    gain = gseq_in[...].reshape(1, W).astype(F32)

    out_row = lax.broadcasted_iota(jnp.int32, (256, 256), 0)
    in_row = lax.broadcasted_iota(jnp.int32, (256, 256), 1)
    perm = (in_row == (out_row & 7) * 32 + (out_row >> 5) * 4 + ((out_row >> 3) & 3)).astype(F32).astype(BF16)

    def first(n):
        start, width = PARTS[n]
        cut = pl.ds(start, width)
        fs, s1, r1 = FS[n], S1[n], R1[n]

        @pl.loop(0, 8, unroll=4)
        def _(o):
            if n == 0:
                r = jnp.concatenate([RR[pl.ds(2 * o, 1), :], RR[pl.ds(2 * o + 1, 1), :]], axis=1)
                SL[o] = (SL[o].astype(F32) * r).astype(BF16)
            rows = X[o, :, :, :, cut].reshape(256, width)
            fs[o] = (dot(SL[o], rows) * gain[:, start : start + width]).astype(BF16)

        @pl.loop(0, 8)
        def _(k):
            g = (k + s // 8) % 8
            block = fs[:, pl.ds(pl.multiple_of(g * 32, 32), 32), :].reshape(256, width)
            s1[pl.ds(g * 8, 8)] = dot(perm, block).astype(BF16).reshape(8, 32, width)

            @pl.loop(0, 8, unroll=8)
            def _(j):
                d = g * 8 + (j + s) % 8

                @pl.when(d != s)
                def _():
                    remote(s1.at[d], r1.at[s], a1_sem.at[0, n], a1_sem.at[1, n], (d, ch)).start()

        r1[s] = s1[s]

    pl.semaphore_wait(met.at[1], 3)
    first(0)
    first(1)
    tokens_across[0].start()
    tokens_across[1].start()

    @pl.loop(0, 16)
    def _(k):
        col = jnp.sum(jnp.where(eye, RR[pl.ds(k, 1), :], 0.0), axis=1, keepdims=True)
        RC[k // 2, pl.ds(2 * (k % 2), 2)] = jnp.broadcast_to(col, (128, 128)).reshape(2, 2, 32, 128)

    for cp in first_unit:
        cp.wait_recv()
    for cp in rings[0]:
        cp.start()
    for cp in rings[0]:
        cp.wait_recv()
    for cp in rings[1]:
        cp.start()
    loads[4].wait()

    def second(n):
        width = PARTS[n][1]
        r1, gb, s2, r2, mb = R1[n], GB[n], S2[n], R2[n], MB[n]
        drain(r1.at[pl.ds(0, 63)], a1_sem.at[1, n])

        @pl.loop(0, 8, unroll=2)
        def _(g):
            part = r1[pl.ds(g * 8, 8)].astype(F32)
            for b in range(4):
                rows = part[:, 8 * b : 8 * b + 8, :].reshape(64, width)
                gb[b, pl.ds(pl.multiple_of(g * 64, 64), 64), :] = rows.astype(BF16)

        low = lax.broadcasted_iota(jnp.int32, (32, 8, width), 1) < 4

        @pl.loop(0, 2)
        def _(k):
            m = (k + y // 2) % 2
            halves = ([], [])
            for pair in range(2):
                even, odd = (
                    dot(SR[b, pl.ds(pl.multiple_of(m * 256, 256), 256), :], gb[b]).reshape(32, 8, width)
                    for b in (2 * pair, 2 * pair + 1)
                )
                halves[0].append(jnp.where(low, even, pltpu.roll(odd, 4, 1)))
                halves[1].append(jnp.where(low, pltpu.roll(even, 4, 1), odd))
            for half in range(2):
                s2[pl.ds(m * 32, 32), half] = jnp.concatenate(halves[half], axis=1).astype(BF16)

            @pl.loop(0, 32, unroll=8)
            def _(j):
                d = m * 32 + (j + s) % 32
                same = (d // 8) % 2 == side

                @pl.when(same & (d != s))
                def _():
                    remote(s2.at[d], r2.at[s], a2_sem.at[0, n], a2_sem.at[1, n], (d, ch)).start()

                @pl.when(jnp.logical_not(same))
                def _():
                    remote(s2.at[d, h], r2.at[s, h], a2_sem.at[0, n], a2_sem.at[1, n], (d, ch)).start()
                    remote(
                        s2.at[d, 1 - h], mb.at[c, y % 2, (l % 2) * 4 + x],
                        mb_sem.at[0, n], mb_sem.at[1, n], (d, far + y // 2),
                    ).start()

        r2[s] = s2[s]

    second(0)
    for cp in rings[1]:
        cp.wait_recv()
    for cp in rings[2]:
        cp.start()
    second(1)
    for cp in rings[2]:
        cp.wait_recv()
    for cp in rings[3]:
        cp.start()

    out_row = lax.broadcasted_iota(jnp.int32, (128, 128), 0)
    in_row = lax.broadcasted_iota(jnp.int32, (128, 128), 1)
    back = (in_row == ((out_row >> 2) & 7) * 16 + (out_row & 3) * 4 + (out_row >> 5)).astype(F32).astype(BF16)

    def streamed(xs, mixed, rc, gains):
        width = xs.shape[-1]
        xs = xs.reshape(128, width).astype(F32)
        rc = jnp.concatenate([rc.reshape(128, 128)] * (width // 128), axis=1)
        normed = (xs * rc * gains).astype(BF16).astype(F32)
        return (xs + dot(back, mixed.reshape(128, width)) * normed).astype(BF16).reshape(4, 32, width)

    def at_home(n, hh, yy, half):
        start, width = PARTS[n]
        o4, cut = pl.ds(4 * hh, 4), pl.ds(start, width)
        mixed = R2[n][pl.ds(yy * 16 + half * 8, 8), hh]
        ST[o4, yy, half, :, cut] = streamed(
            X[o4, yy, half, :, cut], mixed, RC[o4, yy, half], gain[:, start : start + width]
        )

    drain(R2[0].at[pl.ds(0, 47)], a2_sem.at[1, 0])

    @pl.loop(0, 4, unroll=2)
    def _(yy):
        at_home(0, 1 - h, yy, side)

    @pl.loop(0, 8, unroll=2)
    def _(g):
        at_home(0, h, g // 2, g % 2)

    for cp in rings[3]:
        cp.wait_recv()
    for cp in other_block:
        cp.start()
    drain(R2[1].at[pl.ds(0, 47)], a2_sem.at[1, 1])

    @pl.loop(0, 4, unroll=2)
    def _(yy):
        at_home(1, 1 - h, yy, side)

    for t in range(2):
        for k in range(2):
            remote(
                ST.at[pl.ds(2 * far + 2 * t, 2), pl.ds(2 * k, 2), side],
                TS.at[ch, pl.ds(2 * t, 2), :, side],
                st_sem.at[0, t], st_sem.at[1, t], (s, far + k),
            ).start()

    @pl.loop(0, 8, unroll=2)
    def _(g):
        at_home(1, h, g // 2, g % 2)

    for t in range(2):
        remote(
            ST.at[pl.ds(4 * h + 2 * t, 2), pl.ds(2 * (1 - c), 2)], TS.at[ch, pl.ds(2 * t, 2)],
            st_sem.at[0, t], st_sem.at[1, t], to_sib,
        ).start()
    TS[ch] = ST[pl.ds(4 * h, 4), pl.ds(2 * c, 2)]

    drain(G.at[pl.ds(0, 3)], gm_sem.at[1])
    drain(XB, xb_sem.at[1])
    for n, (start, width) in enumerate(PARTS):
        cut = pl.ds(start, width)
        drain(MB[n], mb_sem.at[1, n])
        for k in range(2):
            gains = G[far + k, 0, pl.ds(0, 1), cut].astype(F32)
            for yy in range(2):
                rc = RC[pl.ds(4 * h, 4), 2 * c + yy, 1 - side]
                TS[far + k, :, yy, 1 - side, :, cut] = streamed(XB[k, :, yy, :, cut], MB[n][k, yy], rc, gains)

    for cp in loads[5:]:
        cp.wait()
    for cp in own_block:
        cp.wait_recv()
    for cp in other_block:
        cp.wait_recv()

    def stream_of(i, at):
        return TS[i, at].reshape(128, W).astype(F32)

    @pl.loop(0, 4)
    def _(o):
        t = o // 2
        at = pl.ds(o, 1)

        @pl.when(o % 2 == 0)
        def _():
            drain(TS.at[0], st_sem.at[1, t])

        squares = jnp.zeros((128, 1), F32)
        for i in range(4):
            v = stream_of(i, at)
            squares += jnp.sum(v * v, axis=1, keepdims=True)
        r2 = lax.rsqrt(squares / 1536.0 + EPS)
        projected = []
        for i in range(4):
            n = (stream_of(i, at) * r2 * G[i, 1, pl.ds(0, 1), :].astype(F32)).astype(BF16)
            projected.append([dot(n, UF[i, pl.ds(g * W, W), :]).astype(BF16) for g in range(2)])
        down = []
        for p in range(4):
            merged = [
                jnp.concatenate([projected[i][g][:, p * 128 : p * 128 + 128] for i in range(4)], axis=1) for g in range(2)
            ]
            acc = jnp.zeros((128, 512), F32)
            for n in range(3):
                lanes = pl.ds(n * 512, 512)
                gate, up = (dot(merged[g], US[p, pl.ds(g * 4, 4), :, lanes].reshape(512, 512)) for g in range(2))
                hidden = (gate / (1.0 + jnp.exp(-gate)) * up).astype(BF16)
                acc += dot(hidden, DF[p, pl.ds(n * 512, 512), :])
            down.append(acc.astype(BF16))
        for r in range(4):
            merged = jnp.concatenate([down[p][:, r * 128 : r * 128 + 128] for p in range(4)], axis=1)
            mlp = dot(merged, DS[r].reshape(512, W))
            OB[r, at] = (stream_of(r, at) + mlp).astype(BF16).reshape(1, 2, 2, 32, W)
        home = (pl.ds(4 * h + o, 1), pl.ds(2 * c, 2))
        for r in (far, far + 1, sib):
            remote(OB.at[r, at], out.at[home], out_send.at[t], out_recv.at[t], (s, r)).start()
        pltpu.make_async_copy(OB.at[ch, at], out.at[home], own_sem.at[t]).start()

    drain(SQ.at[pl.ds(0, 3)], sq_sem.at[0])
    drain(G.at[pl.ds(0, 3)], gm_sem.at[0])
    drain(XB, xb_sem.at[0])
    for n in range(2):
        drain(S1[n].at[pl.ds(0, 63)], a1_sem.at[0, n])
        drain(S2[n].at[pl.ds(0, 47)], a2_sem.at[0, n])
        drain(MB[n], mb_sem.at[0, n])
    for cp in first_unit + own_block + other_block + rings[0] + rings[1] + rings[2] + rings[3]:
        cp.wait_send()
    for t in range(2):
        drain(TS.at[0], st_sem.at[0, t])
        drain(out.at[pl.ds(0, 3)], out_send.at[t])
        drain(out.at[pl.ds(0, 3)], out_recv.at[t])
        drain(out.at[pl.ds(0, 1)], own_sem.at[t])


def on_device(
    tokens, norm_gain_seq, seq_left, seq_right, norm_gain_mlp, up_first, up_second, down_first, down_second
):
    rows = tokens.shape[0]
    hbm = pl.BlockSpec(memory_space=pl.ANY)
    vmem = pl.BlockSpec(memory_space=pltpu.VMEM)
    dma = pltpu.SemaphoreType.DMA
    out = pl.pallas_call(
        layer_kernel,
        out_shape=jax.ShapeDtypeStruct((8, 4, 2, 32, W), BF16),
        in_specs=[hbm, vmem, vmem] + [hbm] * 6,
        out_specs=hbm,
        scratch_shapes=[
            pltpu.VMEM((8, 4, 2, 32, W), BF16),
            pltpu.VMEM((4, 2, 16, W), BF16),
            pltpu.VMEM((8, 256, 256), BF16),
            pltpu.VMEM((4, 512, 512), BF16),
            pltpu.VMEM((4, 16, 128), F32),
            pltpu.VMEM((16, 128), F32),
            pltpu.VMEM((8, 4, 2, 32, 128), F32),
            *[pltpu.VMEM((8, 256, w), BF16) for _, w in PARTS],
            *[pltpu.VMEM((64, 32, w), BF16) for _, w in PARTS],
            *[pltpu.VMEM((64, 32, w), BF16) for _, w in PARTS],
            *[pltpu.VMEM((4, 512, w), BF16) for _, w in PARTS],
            *[pltpu.VMEM((64, 2, 16, w), BF16) for _, w in PARTS],
            *[pltpu.VMEM((64, 2, 16, w), BF16) for _, w in PARTS],
            *[pltpu.VMEM((2, 2, 8, 16, w), BF16) for _, w in PARTS],
            pltpu.VMEM((2, 4, 2, 32, W), BF16),
            pltpu.VMEM((8, 4, 2, 32, W), BF16),
            pltpu.VMEM((4, 4, 2, 2, 32, W), BF16),
            pltpu.VMEM((4, 4, 2, 2, 32, W), BF16),
            pltpu.VMEM((4, 768, 512), BF16),
            pltpu.VMEM((4, 8, 128, 1536), BF16),
            pltpu.VMEM((4, 1536, 512), BF16),
            pltpu.VMEM((4, 4, 128, W), BF16),
            pltpu.VMEM((768, W), BF16),
            pltpu.VMEM((1536, W), BF16),
            pltpu.SemaphoreType.REGULAR((2,)),
            dma((7,)), dma((2,)), dma((2,)), dma((2,)), dma((2, 2)), dma((2, 2)), dma((2, 2)), dma((2, 2)), dma((2,)), dma((2,)), dma((2,)),
            dma((4,)), dma((4,)), dma((32,)), dma((32,)), dma((8,)), dma((8,)),
        ],
        compiler_params=pltpu.CompilerParams(
            collective_id=0, has_side_effects=True, vmem_limit_bytes=60 * 2**20
        ),
        name="layer",
    )(
        tokens.reshape(8, 4, 2, 32, W), norm_gain_seq, norm_gain_mlp, seq_left, seq_right, up_first.reshape(768, W),
        up_second.reshape(8, 96, 1536), down_first.reshape(1536, W), down_second.reshape(4, 96, W),
    )
    return out.reshape(rows, 1, W)


def solution(mesh):
    return jax.shard_map(
        on_device,
        mesh=mesh,
        in_specs=(
            P("seq", None, "chan"),
            P("chan"),
            P("seq", None, None),
            P("seq", None, None),
            P("chan"),
            P(None, "chan", None, None),
            P(None, "chan", None, None),
            P("chan", None, None),
            P("chan", None, None),
        ),
        out_specs=P("seq", None, "chan"),
        check_vma=False,
    )
```
